32 devices in a mesh: parts: 1, replica: 32 (over z, y, x, core).
Axes of the slice: x: 2, y: 2, z: 4, core: 2. Of those that a mesh axis runs over, the one named last changes fastest.
Arguments:
- attention_output: bfloat16 [152, 8192], P('parts', 'replica'), may hold values from -6 to 6
- output_weight: bfloat16 [8192, 8192], P('replica'), may hold values from -0.0625 to 0.0625
- down_weight: bfloat16 [128, 8192, 64], P(('parts', 'replica')), may hold values from -0.0625 to 0.0625
- up_weight: bfloat16 [128, 8192, 64], P(('parts', 'replica')), may hold values from -0.75 to 0.75
- store_adapter_ids: int32 [128], P('parts'), may hold values from 0 to 127, as said below
- segment_adapter: int32 [8], P('parts'), may hold values from 0 to 127, as said below
- segment_rows: int32 [8], P('parts'), may hold values from 1 to 32, 128 in all
Outputs:
- mixed: bfloat16 [152, 8192], P('parts', 'replica')
The draws below stay inside these ranges and needn't reach their ends.
Inputs may be any that keep to these rules, and one draw needn't show every extreme that they name: `store_adapter_ids`: a permutation; device r of the replica axis holds store slots r * 4 to r * 4 + 3. `segment_adapter`: 8 different adapters; at most 2 of them lie in one device's store slots, and some device's store holds exactly 2 of them. `segment_rows`: the counts sum to 128.
All inputs are finite; a program needn't handle non-finite values.
Results may differ from the reference program's by a relative error of at most 0.0046.
Values may be sent and summed in bfloat16 or wider, within the bound.
No kernel may reach another device: no remote copies, remote signals or barrier semaphores. Data moves between devices by JAX's collectives and lax.ppermute only.
A program may use at most 128 MiB of HBM per device.

```python
import math
import jax
import jax.numpy as jnp
import numpy as np
from jax import lax

MODEL_FEATURES = 8192
ADAPTER_RANK = 64
ADP_DEV = 4
BLOCK = 4
ROWS = 128
STORE_ADAPTERS = 128
NSEG = 8
MOST = 32
PROWS = 152
N_REPLICA = 32


def swap_labels(values, first, second):
    return jnp.where(values == first, second, jnp.where(values == second, first, values)).astype(jnp.int32)


def choose_adapters(key):
    stored = jax.random.permutation(key, STORE_ADAPTERS).astype(jnp.int32)
    key = jax.random.fold_in(key, 7)
    key_owner, key_slot, key_shuffle = jax.random.split(key, 3)
    owners = jax.random.permutation(key_owner, N_REPLICA).astype(jnp.int32)
    pair_count = NSEG // 4
    single_count = NSEG - 2 * pair_count
    scores = jax.random.randint(key_slot, (N_REPLICA, ADP_DEV), 0, 2 ** 20) * ADP_DEV
    scores = scores + jnp.arange(ADP_DEV, dtype=jnp.int32)[None, :]
    slot_order = jnp.argsort(scores, axis=1).astype(jnp.int32)
    first_owners = owners[:pair_count + single_count]
    second_owners = owners[:pair_count]
    first_slots = first_owners * ADP_DEV + slot_order[first_owners, 0]
    second_slots = second_owners * ADP_DEV + slot_order[second_owners, 1]
    slot_list = jnp.concatenate([first_slots, second_slots])
    shuffle = jax.random.permutation(key_shuffle, NSEG)
    chosen = stored[slot_list][shuffle].astype(jnp.int32)
    highest = jnp.max(chosen)
    stored = swap_labels(stored, highest, STORE_ADAPTERS - 1)
    chosen = swap_labels(chosen, highest, STORE_ADAPTERS - 1)
    lowest = jnp.min(chosen)
    stored = swap_labels(stored, lowest, 0)
    chosen = swap_labels(chosen, lowest, 0)
    return (stored, chosen)


def draw_store_adapter_ids(key, part):
    return choose_adapters(key)[0]


def draw_segment_adapter(key, part):
    return choose_adapters(key)[1]


def steps_of(stream_key, dims, shards, least, largest):
    def one(axis_at, blocks):
        heights = jax.random.uniform(jax.random.fold_in(jax.random.fold_in(stream_key, 6), axis_at), (blocks,), jnp.float32, least / len(shards), largest / len(shards))
        return jnp.repeat(jnp.exp(heights), dims[axis_at] // blocks).reshape((-1,) + (1,) * (len(dims) - axis_at - 1))

    factor_of = one(*shards[0])
    for cut in shards[1:]:
        factor_of = factor_of * one(*cut)
    return factor_of


def split_up(count, total, reach, skew):
    weights = [(1 << 20) // math.isqrt(standing ** skew) + 1 for standing in range(2, count + 1)]
    rest, holding = total - reach - (count - 1), [1] * (count - 1)
    while rest > 0:
        movable = [i for i in range(count - 1) if holding[i] < reach]
        whole, left = sum([weights[i] for i in movable]), rest
        for i in movable:
            extra = min(reach - holding[i], max(1, left * weights[i] // whole), rest)
            holding[i] = holding[i] + extra
            rest = rest - extra
    return np.array([reach] + holding)


def ragged(rng, amount, total, most, lean):
    if amount == 2:
        one = jax.random.randint(rng, (), max(1, total - most), min(most, total - 1) + 1)
        return jnp.stack([one, total - one])
    tallies = jnp.asarray(split_up(amount, total, most, lean), jnp.int32)
    couples = (amount - 1) // 2
    giver, sink = tallies[1:1 + 2 * couples:2], tallies[2:2 + 2 * couples:2]
    margin = jnp.minimum(giver - 1, most - sink)
    shifted = jax.random.randint(jax.random.fold_in(rng, 1), (couples,), 0, 1 << 20) % (margin + 1)
    tallies = tallies.at[1:1 + 2 * couples:2].set(giver - shifted).at[2:2 + 2 * couples:2].set(sink + shifted)
    return tallies[jax.random.permutation(jax.random.fold_in(rng, 2), amount)]


def centred(stream_key, extent, scale, reach, shards=(), held_as=jnp.bfloat16):
    drawn = scale * jax.random.normal(stream_key, extent, jnp.float32)
    if shards:
        drawn = drawn * steps_of(stream_key, extent, shards, -0.22, 0.18)
    return jnp.clip(drawn, -reach, reach).astype(held_as)


def setup_inputs(seed: int = 0, part: int = 0) -> dict:
    arg_keys = jax.random.split(jax.random.key(seed), 8)
    own_keys = jax.random.split(jax.random.fold_in(arg_keys[7], part), 8)
    return {
        "attention_output": centred(own_keys[0], (PROWS, MODEL_FEATURES), 1.0, 6.0, ((1, 32),)),
        "output_weight": centred(arg_keys[1], (MODEL_FEATURES, MODEL_FEATURES), MODEL_FEATURES ** -0.5, 0.0625, ((0, 32),)),
        "down_weight": centred(own_keys[2], (STORE_ADAPTERS, MODEL_FEATURES, ADAPTER_RANK), MODEL_FEATURES ** -0.5, 0.0625, ((0, 32),)),
        "up_weight": centred(own_keys[3], (STORE_ADAPTERS, MODEL_FEATURES, ADAPTER_RANK), ADAPTER_RANK ** -0.5, 0.75, ((0, 32),)),
        "store_adapter_ids": draw_store_adapter_ids(jax.random.fold_in(jax.random.fold_in(arg_keys[7], part), 71), part),
        "segment_adapter": draw_segment_adapter(jax.random.fold_in(jax.random.fold_in(arg_keys[7], part), 71), part),
        "segment_rows": ragged(own_keys[6], NSEG, ROWS, MOST, 2).astype(jnp.int32),
    }


ADAPTER_SCALE = 2.0


def segment_member(segment_rows, total_rows, block_rows):
    padded = ((segment_rows + block_rows - 1) // block_rows) * block_rows
    starts = jnp.cumsum(padded) - padded
    row_ids = jnp.arange(total_rows, dtype=jnp.int32)
    inside = (row_ids[:, None] >= starts[None, :]) & (row_ids[:, None] < (starts + segment_rows)[None, :])
    return inside.astype(jnp.float32)


def slot_lookup(store_adapter_ids, segment_adapter):
    positions = jnp.arange(store_adapter_ids.shape[0], dtype=jnp.int32)
    equal = store_adapter_ids[None, :] == segment_adapter[:, None]
    return jnp.sum(jnp.where(equal, positions[None, :], 0), axis=1).astype(jnp.int32)


def reference(attention_output, output_weight, down_weight, up_weight, store_adapter_ids, segment_adapter, segment_rows):
    member = segment_member(segment_rows, PROWS, BLOCK)
    active_rows = jnp.sum(member, axis=1)
    slot_for_adapter = slot_lookup(store_adapter_ids, segment_adapter)
    base_complete = jnp.dot(attention_output, output_weight, preferred_element_type=jnp.float32)
    down_selected = down_weight[slot_for_adapter].astype(jnp.float32)
    up_selected = up_weight[slot_for_adapter].astype(jnp.float32)
    shrink_all = jnp.einsum('pd,sdr->psr', attention_output.astype(jnp.float32), down_selected, precision=lax.Precision.HIGHEST)
    shrink = jnp.einsum('ps,psr->pr', member, shrink_all, precision=lax.Precision.HIGHEST)
    shrink_half = shrink.astype(jnp.bfloat16)
    spread = member[:, :, None] * shrink_half.astype(jnp.float32)[:, None, :]
    spread = spread.reshape(PROWS, NSEG * ADAPTER_RANK)
    b_matrix = jnp.transpose(up_selected, (0, 2, 1)).reshape(NSEG * ADAPTER_RANK, MODEL_FEATURES)
    adapter_contribution = jnp.dot(spread, b_matrix, precision=lax.Precision.HIGHEST)
    mixed = active_rows[:, None] * (base_complete + ADAPTER_SCALE * adapter_contribution)
    return mixed.astype(jnp.bfloat16)
```

```python
import jax
import jax.numpy as jnp
from jax import lax
from jax.experimental import pallas as pl
from jax.experimental.pallas import tpu as pltpu
from jax.sharding import PartitionSpec as P

BLOCK = 4


ADAPTER_SCALE = 2.0

CHUNKS = 1

PICKED = 2

VMEM_LIMIT = 40 * 1024 * 1024


def segment_member(segment_rows, total_rows, block_rows):
    padded = (segment_rows + block_rows - 1) // block_rows * block_rows
    starts = jnp.cumsum(padded) - padded
    row_ids = jnp.arange(total_rows, dtype=jnp.int32)
    inside = (row_ids[:, None] >= starts[None, :]) & (
        row_ids[:, None] < (starts + segment_rows)[None, :]
    )
    return inside.astype(jnp.float32)


def slot_lookup(store_adapter_ids, segment_adapter):
    positions = jnp.arange(store_adapter_ids.shape[0], dtype=jnp.int32)
    equal = store_adapter_ids[None, :] == segment_adapter[:, None]
    return jnp.sum(jnp.where(equal, positions[None, :], 0), axis=1)


def tile_side(
    attention_output,
    output_weight,
    down_weight,
    up_weight,
    store_adapter_ids,
    segment_adapter,
    segment_rows,
):
    device_list = lax.axis_size("replica")
    total_rows, feature_columns = attention_output.shape
    holding_count, hidden_width, adapter_rank_size = down_weight.shape
    seg_count = segment_rows.shape[0]
    member = segment_member(segment_rows, total_rows, BLOCK)
    active_rows = jnp.sum(member, axis=1)
    slot_for_adapter = slot_lookup(store_adapter_ids, segment_adapter)
    partial_value = jnp.dot(attention_output, output_weight, preferred_element_type=jnp.float32)
    down_pieces = down_weight.reshape(
        holding_count, device_list, feature_columns, adapter_rank_size
    )
    up_pieces = up_weight.reshape(holding_count, device_list, feature_columns, adapter_rank_size)
    tile_pairs = jnp.concatenate([down_pieces, up_pieces], axis=3)
    arrived = lax.all_to_all(tile_pairs, "replica", split_axis=1, concat_axis=0, tiled=True)
    arrived = arrived.reshape(-1, feature_columns, 2 * adapter_rank_size)
    seg_tiles = arrived[slot_for_adapter]
    a_part = seg_tiles[:, :, :adapter_rank_size]
    b_part = seg_tiles[:, :, adapter_rank_size:]
    a_matrix = jnp.transpose(a_part, (1, 0, 2)).reshape(
        feature_columns, seg_count * adapter_rank_size
    )
    shrink_all = jnp.dot(attention_output, a_matrix, preferred_element_type=jnp.float32)
    shrink_all = shrink_all.reshape(total_rows, seg_count, adapter_rank_size)
    shrink_part = jnp.einsum("ps,psr->pr", member, shrink_all)
    base_column_block = lax.psum_scatter(partial_value, "replica", scatter_dimension=1, tiled=True)
    shrink = lax.psum(shrink_part, "replica")
    shrink_half = shrink.astype(jnp.bfloat16)
    spread = (member[:, :, None] * shrink_half.astype(jnp.float32)[:, None, :]).astype(jnp.bfloat16)
    spread = spread.reshape(total_rows, seg_count * adapter_rank_size)
    b_matrix = jnp.transpose(b_part, (0, 2, 1)).reshape(
        seg_count * adapter_rank_size, feature_columns
    )
    adapter_column_block = jnp.dot(spread, b_matrix, preferred_element_type=jnp.float32)
    mixed = active_rows[:, None] * (base_column_block + ADAPTER_SCALE * adapter_column_block)
    return mixed.astype(jnp.bfloat16)


def stage_masks(device_count):
    masks = []
    mask = device_count // 2
    while mask >= 2:
        masks.append(mask)
        mask //= 2
    other = list(masks)
    if len(other) >= 2:
        other[-1], other[-2] = other[-2], other[-1]
    return masks, other


def position_masks(masks):
    found = [0]
    for mask in masks:
        found = found + [value ^ mask for value in found]
    return found


def exchange(value, mask_even, mask_odd):
    count = lax.axis_size("replica")
    pairs = [(i, i ^ (mask_odd if i & 1 else mask_even)) for i in range(count)]
    return lax.ppermute(value, "replica", pairs)


def block_at(device, position, tables):
    even, odd = tables[0][position], tables[1][position]
    if even == odd:
        return jnp.bitwise_xor(device, even)
    return jnp.bitwise_xor(device, jnp.where(jnp.bitwise_and(device, 1) == 0, even, odd))


def padded_row(live_row, rows_ref):
    place = live_row
    end = jnp.int32(0)
    for s in range(rows_ref.shape[0]):
        count = rows_ref[s]
        gap = (BLOCK - count % BLOCK) % BLOCK
        end = end + count
        place = place + jnp.where(live_row >= end, gap, 0)
    return place


def compact_kernel(rows_ref, x_ref, *out_refs):
    step = out_refs[0].shape[0]
    live_rows = step * len(out_refs)
    shape = (live_rows, x_ref.shape[0])
    live_row = lax.broadcasted_iota(jnp.int32, shape, 0)
    layout_row = lax.broadcasted_iota(jnp.int32, shape, 1)
    pick = jnp.where(padded_row(live_row, rows_ref) == layout_row, 1.0, 0.0).astype(jnp.bfloat16)
    rows = jnp.dot(pick, x_ref[...], preferred_element_type=jnp.float32).astype(jnp.bfloat16)
    for i, out_ref in enumerate(out_refs):
        out_ref[...] = rows[i * step : (i + 1) * step]


def spread_rows_kernel(count, rows_ref, *refs):
    keep_refs, got_refs, out_ref = refs[:count], refs[count : 2 * count], refs[2 * count]
    live = [
        (k[0] + g[0].astype(jnp.float32)).astype(jnp.bfloat16) for k, g in zip(keep_refs, got_refs)
    ]
    mixed = live[0] if count == 1 else jnp.concatenate(live, axis=0)
    shape = (out_ref.shape[0], mixed.shape[0])
    live_row = lax.broadcasted_iota(jnp.int32, shape, 1)
    layout_row = lax.broadcasted_iota(jnp.int32, shape, 0)
    pick = jnp.where(padded_row(live_row, rows_ref) == layout_row, 1.0, 0.0).astype(jnp.bfloat16)
    out_ref[...] = jnp.dot(pick, mixed, preferred_element_type=jnp.float32).astype(jnp.bfloat16)


def base_kernel(tables, chunks, info_ref, *refs):
    x_refs, w_ref, send_ref, keep_ref = refs[:chunks], refs[chunks], refs[chunks + 1], refs[chunks + 2]
    me = info_ref[0]
    peer = jnp.bitwise_xor(me, 1)
    x = jnp.concatenate([x_ref[...] for x_ref in x_refs], axis=0) if chunks > 1 else x_refs[0][...]
    width = x.shape[1]
    for p in range(len(tables[0])):
        for device, out_ref in ((peer, send_ref), (me, keep_ref)):
            at = pl.multiple_of(block_at(device, p, tables) * width, width)
            part = jnp.dot(x, w_ref[:, pl.ds(at, width)], preferred_element_type=jnp.float32)
            out_ref[p] = part.astype(out_ref.dtype)


def tiles_kernel(tables, info_ref, down_ref, up_ref, down_send, up_send, down_keep, up_keep):
    me = info_ref[0]
    peer = jnp.bitwise_xor(me, 1)
    width = down_keep.shape[2]
    for p in range(len(tables[0])):
        for device, down_out, up_out in ((peer, down_send, up_send), (me, down_keep, up_keep)):
            at = pl.multiple_of(block_at(device, p, tables) * width, width)
            down_out[p] = down_ref[0, :, pl.ds(at, width)]
            up_out[p] = up_ref[0, :, pl.ds(at, width)]


def row_codes(first_row, shape, info_ref, rows_ref):
    live_row = lax.broadcasted_iota(jnp.int32, shape, 0) + first_row
    code = jnp.zeros(shape, jnp.int32)
    start = jnp.int32(0)
    for s in range(rows_ref.shape[0]):
        end = start + rows_ref[s]
        code = jnp.where((live_row >= start) & (live_row < end), info_ref[1 + PICKED + s], code)
        start = end
    return code


def shrink_kernel(first_row, info_ref, rows_ref, x_ref, own_ref, peer_ref, out_ref):
    positions, rows, _ = x_ref.shape
    rank = out_ref.shape[1]
    contract = (((1,), (1,)), ((), ()))
    own = jnp.zeros((rows, own_ref.shape[1]), jnp.float32)
    peer = jnp.zeros((rows, own_ref.shape[1]), jnp.float32)
    for p in range(positions):
        x = x_ref[p]
        own = own + lax.dot_general(x, own_ref[p], contract, preferred_element_type=jnp.float32)
        peer = peer + lax.dot_general(x, peer_ref[p], contract, preferred_element_type=jnp.float32)
    code = row_codes(first_row, (rows, rank), info_ref, rows_ref)
    total = jnp.zeros((rows, rank), jnp.float32)
    for place, part in enumerate((own, peer)):
        for j in range(PICKED):
            value = part[:, j * rank : (j + 1) * rank]
            total = total + jnp.where(code == 1 + place * PICKED + j, value, 0.0)
    out_ref[...] = total


def expand_kernel(
    first_row, info_ref, rows_ref, mine_ref, got_ref, keep_ref, base_ref, own_ref, peer_ref, out_ref
):
    rows, rank = mine_ref.shape
    half = (mine_ref[...] + got_ref[...]).astype(jnp.bfloat16)
    code = row_codes(first_row, (rows, rank), info_ref, rows_ref)
    picked = [
        jnp.where(code == 1 + j, half.astype(jnp.float32), 0.0).astype(jnp.bfloat16)
        for j in range(2 * PICKED)
    ]
    own = jnp.concatenate(picked[:PICKED], axis=1)
    peer = jnp.concatenate(picked[PICKED:], axis=1)
    for p in range(out_ref.shape[0]):
        term = jnp.dot(own, own_ref[p], preferred_element_type=jnp.float32)
        term = term + jnp.dot(peer, peer_ref[p], preferred_element_type=jnp.float32)
        base = keep_ref[p] + base_ref[p].astype(jnp.float32)
        out_ref[p] = (base + ADAPTER_SCALE * term).astype(out_ref.dtype)


def smem():
    return pl.BlockSpec(memory_space=pltpu.SMEM)


def vmem():
    return pl.BlockSpec(memory_space=pltpu.VMEM)


def params(**more):
    return pltpu.CompilerParams(vmem_limit_bytes=VMEM_LIMIT, **more)


def owner_side(
    attention_output,
    output_weight,
    down_weight,
    up_weight,
    store_adapter_ids,
    segment_adapter,
    segment_rows,
):
    bf16, f32 = jnp.bfloat16, jnp.float32
    device_count = lax.axis_size("replica")
    me = lax.axis_index("replica")
    total_rows, width = attention_output.shape
    held, _, rank = down_weight.shape
    seg_count = segment_rows.shape[0]
    live_rows = total_rows - seg_count * (BLOCK - 1)
    step = live_rows // CHUNKS
    even_masks, odd_masks = stage_masks(device_count)
    tables = (position_masks(even_masks), position_masks(odd_masks))
    positions = len(tables[0])

    slot = slot_lookup(store_adapter_ids, segment_adapter)
    owner, local = slot // held, slot % held

    def picks(device):
        here = owner == device
        low = jnp.minimum(jnp.min(jnp.where(here, local, held)), held - 1)
        high = jnp.max(jnp.where(here, local, 0))
        return here, low, high

    own_here, own_low, own_high = picks(me)
    peer_here, peer_low, _ = picks(me ^ 1)
    place = jnp.where(own_here, jnp.where(local == own_low, 1, 2), 0)
    place = jnp.where(peer_here, PICKED + jnp.where(local == peer_low, 1, 2), place)
    info = jnp.concatenate([jnp.stack([me, own_low, own_high]), place]).astype(jnp.int32)

    live = pl.pallas_call(
        compact_kernel,
        out_shape=[jax.ShapeDtypeStruct((step, width), bf16)] * CHUNKS,
        in_specs=[smem(), vmem()],
        out_specs=[vmem()] * CHUNKS,
        compiler_params=params(),
        name="compact_rows",
    )(segment_rows, attention_output)

    tile = jax.ShapeDtypeStruct((positions, PICKED * rank, width), bf16)
    tile_in = pl.BlockSpec((1, rank, down_weight.shape[1]), lambda j, info: (info[1 + j], 0, 0))
    tile_out = pl.BlockSpec((positions, rank, width), lambda j, info: (0, j, 0))
    down_send, up_send, down_own, up_own = pl.pallas_call(
        lambda *refs: tiles_kernel(tables, *refs),
        out_shape=[tile] * 4,
        grid_spec=pltpu.PrefetchScalarGridSpec(
            num_scalar_prefetch=1,
            grid=(PICKED,),
            in_specs=[tile_in, tile_in],
            out_specs=[tile_out] * 4,
        ),
        compiler_params=params(dimension_semantics=("arbitrary",)),
        name="cut_tiles",
    )(info, jnp.transpose(down_weight, (0, 2, 1)), jnp.transpose(up_weight, (0, 2, 1)))
    down_peer = exchange(down_send, 1, 1)
    up_peer = exchange(up_send, 1, 1)

    base_send, base_keep = pl.pallas_call(
        lambda *refs: base_kernel(tables, CHUNKS, *refs),
        out_shape=[
            jax.ShapeDtypeStruct((positions, live_rows, width), bf16),
            jax.ShapeDtypeStruct((positions, live_rows, width), f32),
        ],
        in_specs=[smem()] + [vmem()] * (CHUNKS + 1),
        out_specs=[vmem()] * 2,
        compiler_params=params(),
        name="base_partials",
    )(info, *live, output_weight)
    base_got = exchange(base_send, 1, 1)

    gathered = [part[None] for part in live]
    for mask_even, mask_odd in zip(even_masks, odd_masks):
        got = [exchange(part, mask_even, mask_odd) for part in gathered]
        gathered = [jnp.concatenate(pair, axis=0) for pair in zip(gathered, got)]

    half = positions // 2
    totals = []
    for i in range(CHUNKS):
        mine = pl.pallas_call(
            lambda *refs, i=i: shrink_kernel(i * step, *refs),
            out_shape=jax.ShapeDtypeStruct((step, rank), f32),
            in_specs=[smem()] * 2 + [vmem()] * 3,
            out_specs=vmem(),
            compiler_params=params(),
            name="shrink",
        )(info, segment_rows, gathered[i], down_own, down_peer)
        got = exchange(mine, 1, 1)

        def expand(part, dtype, i=i, mine=mine, got=got):
            whole = pl.BlockSpec((step, rank), lambda g: (0, 0))
            rows_of = pl.BlockSpec((half, step, width), lambda g: (part, i, 0))
            tiles_of = pl.BlockSpec((half, PICKED * rank, width), lambda g: (part, 0, 0))
            return pl.pallas_call(
                lambda *refs: expand_kernel(i * step, *refs),
                grid=(1,),
                out_shape=jax.ShapeDtypeStruct((half, step, width), dtype),
                in_specs=[smem()] * 2 + [whole] * 2 + [rows_of] * 2 + [tiles_of] * 2,
                out_specs=pl.BlockSpec((half, step, width), lambda g: (0, 0, 0)),
                compiler_params=params(dimension_semantics=("arbitrary",)),
                name="expand",
            )(info, segment_rows, mine, got, base_keep, base_got, up_own, up_peer)

        totals.append((expand(0, f32), expand(1, bf16)))

    keep = [pair[0] for pair in totals]
    send = [pair[1] for pair in totals]
    got = None
    for k, (mask_even, mask_odd) in enumerate(zip(reversed(even_masks), reversed(odd_masks))):
        if k:
            left = keep[0].shape[0] // 2
            sums = [a + b.astype(f32) for a, b in zip(keep, got)]
            keep = [value[:left] for value in sums]
            send = [value[left:].astype(bf16) for value in sums]
        got = [exchange(value, mask_even, mask_odd) for value in send]
    return pl.pallas_call(
        lambda *refs: spread_rows_kernel(CHUNKS, *refs),
        out_shape=jax.ShapeDtypeStruct((total_rows, width), bf16),
        in_specs=[smem()] + [vmem()] * (2 * CHUNKS),
        out_specs=vmem(),
        compiler_params=params(),
        name="spread_rows",
    )(segment_rows, *keep, *got)


def per_device(*arrays):
    width, features = arrays[0].shape[1], arrays[1].shape[1]
    if width % 128 == 0 and lax.axis_size("replica") >= 4:
        return owner_side(*arrays)
    return tile_side(*arrays)


def solution(mesh):
    in_specs = (
        P("parts", "replica"),
        P("replica", None),
        P(("parts", "replica"), None, None),
        P(("parts", "replica"), None, None),
        P("parts"),
        P("parts"),
        P("parts"),
    )
    out_specs = P("parts", "replica")
    return jax.shard_map(
        per_device, mesh=mesh, in_specs=in_specs, out_specs=out_specs, check_vma=False
    )
```

```python
import jax
import jax.numpy as jnp
from jax import lax
from jax.experimental import pallas as pl
from jax.experimental.pallas import tpu as pltpu
from jax.sharding import PartitionSpec as P

BLOCK = 4


ADAPTER_SCALE = 2.0

CHUNKS = 2

PICKED = 2

VMEM_LIMIT = 40 * 1024 * 1024


def segment_member(segment_rows, total_rows, block_rows):
    padded = (segment_rows + block_rows - 1) // block_rows * block_rows
    starts = jnp.cumsum(padded) - padded
    row_ids = jnp.arange(total_rows, dtype=jnp.int32)
    inside = (row_ids[:, None] >= starts[None, :]) & (
        row_ids[:, None] < (starts + segment_rows)[None, :]
    )
    return inside.astype(jnp.float32)


def slot_lookup(store_adapter_ids, segment_adapter):
    positions = jnp.arange(store_adapter_ids.shape[0], dtype=jnp.int32)
    equal = store_adapter_ids[None, :] == segment_adapter[:, None]
    return jnp.sum(jnp.where(equal, positions[None, :], 0), axis=1)


def tile_side(
    attention_output,
    output_weight,
    down_weight,
    up_weight,
    store_adapter_ids,
    segment_adapter,
    segment_rows,
):
    device_list = lax.axis_size("replica")
    total_rows, feature_columns = attention_output.shape
    holding_count, hidden_width, adapter_rank_size = down_weight.shape
    seg_count = segment_rows.shape[0]
    member = segment_member(segment_rows, total_rows, BLOCK)
    active_rows = jnp.sum(member, axis=1)
    slot_for_adapter = slot_lookup(store_adapter_ids, segment_adapter)
    partial_value = jnp.dot(attention_output, output_weight, preferred_element_type=jnp.float32)
    down_pieces = down_weight.reshape(
        holding_count, device_list, feature_columns, adapter_rank_size
    )
    up_pieces = up_weight.reshape(holding_count, device_list, feature_columns, adapter_rank_size)
    tile_pairs = jnp.concatenate([down_pieces, up_pieces], axis=3)
    arrived = lax.all_to_all(tile_pairs, "replica", split_axis=1, concat_axis=0, tiled=True)
    arrived = arrived.reshape(-1, feature_columns, 2 * adapter_rank_size)
    seg_tiles = arrived[slot_for_adapter]
    a_part = seg_tiles[:, :, :adapter_rank_size]
    b_part = seg_tiles[:, :, adapter_rank_size:]
    a_matrix = jnp.transpose(a_part, (1, 0, 2)).reshape(
        feature_columns, seg_count * adapter_rank_size
    )
    shrink_all = jnp.dot(attention_output, a_matrix, preferred_element_type=jnp.float32)
    shrink_all = shrink_all.reshape(total_rows, seg_count, adapter_rank_size)
    shrink_part = jnp.einsum("ps,psr->pr", member, shrink_all)
    base_column_block = lax.psum_scatter(partial_value, "replica", scatter_dimension=1, tiled=True)
    shrink = lax.psum(shrink_part, "replica")
    shrink_half = shrink.astype(jnp.bfloat16)
    spread = (member[:, :, None] * shrink_half.astype(jnp.float32)[:, None, :]).astype(jnp.bfloat16)
    spread = spread.reshape(total_rows, seg_count * adapter_rank_size)
    b_matrix = jnp.transpose(b_part, (0, 2, 1)).reshape(
        seg_count * adapter_rank_size, feature_columns
    )
    adapter_column_block = jnp.dot(spread, b_matrix, preferred_element_type=jnp.float32)
    mixed = active_rows[:, None] * (base_column_block + ADAPTER_SCALE * adapter_column_block)
    return mixed.astype(jnp.bfloat16)


def stage_masks(device_count):
    masks = []
    mask = device_count // 2
    while mask >= 2:
        masks.append(mask)
        mask //= 2
    other = list(masks)
    if len(other) >= 2:
        other[-1], other[-2] = other[-2], other[-1]
    return masks, other


def position_masks(masks):
    found = [0]
    for mask in masks:
        found = found + [value ^ mask for value in found]
    return found


def exchange(value, mask_even, mask_odd):
    count = lax.axis_size("replica")
    pairs = [(i, i ^ (mask_odd if i & 1 else mask_even)) for i in range(count)]
    return lax.ppermute(value, "replica", pairs)


def block_at(device, position, tables):
    even, odd = tables[0][position], tables[1][position]
    if even == odd:
        return jnp.bitwise_xor(device, even)
    return jnp.bitwise_xor(device, jnp.where(jnp.bitwise_and(device, 1) == 0, even, odd))


def padded_row(live_row, rows_ref):
    place = live_row
    end = jnp.int32(0)
    for s in range(rows_ref.shape[0]):
        count = rows_ref[s]
        gap = (BLOCK - count % BLOCK) % BLOCK
        end = end + count
        place = place + jnp.where(live_row >= end, gap, 0)
    return place


def compact_kernel(chunks, rows_hbm, x_hbm, *refs):
    out_refs, pick_ref, code_ref = refs[:chunks], refs[chunks], refs[chunks + 1]
    rows_ref, x_ref, rows_sem, x_sem = refs[chunks + 2 :]
    x_copy = pltpu.make_async_copy(x_hbm, x_ref, x_sem)
    x_copy.start()
    rows_copy = pltpu.make_async_copy(rows_hbm, rows_ref, rows_sem)
    rows_copy.start()
    rows_copy.wait()
    step = out_refs[0].shape[0]
    shape = (step * chunks, x_ref.shape[0])
    live_row = lax.broadcasted_iota(jnp.int32, shape, 0)
    layout_row = lax.broadcasted_iota(jnp.int32, shape, 1)
    pick = jnp.where(padded_row(live_row, rows_ref) == layout_row, 1.0, 0.0).astype(jnp.bfloat16)
    x_copy.wait()
    rows = jnp.dot(pick, x_ref[...], preferred_element_type=jnp.float32).astype(jnp.bfloat16)
    for i, out_ref in enumerate(out_refs):
        out_ref[...] = rows[i * step : (i + 1) * step]
    shape = pick_ref.shape
    live_row = lax.broadcasted_iota(jnp.int32, shape, 1)
    layout_row = lax.broadcasted_iota(jnp.int32, shape, 0)
    back = padded_row(live_row, rows_ref) == layout_row
    pick_ref[...] = jnp.where(back, 1.0, 0.0).astype(jnp.bfloat16)
    live_row = lax.broadcasted_iota(jnp.int32, code_ref.shape, 0)
    segment = jnp.zeros(code_ref.shape, jnp.int32)
    end = jnp.int32(0)
    for s in range(rows_ref.shape[0] - 1):
        end = end + rows_ref[s]
        segment = segment + jnp.where(live_row >= end, 1, 0)
    code_ref[...] = segment


def spread_rows_kernel(count, pick_ref, *refs):
    keep_refs, got_refs, out_ref = refs[:count], refs[count : 2 * count], refs[2 * count]
    live = [
        (k[0] + g[0].astype(jnp.float32)).astype(jnp.bfloat16) for k, g in zip(keep_refs, got_refs)
    ]
    mixed = live[0] if count == 1 else jnp.concatenate(live, axis=0)
    out = jnp.dot(pick_ref[...], mixed, preferred_element_type=jnp.float32)
    out_ref[...] = out.astype(jnp.bfloat16)


def base_kernel(tables, chunks, info_ref, *refs):
    x_refs, w_ref, send_ref, keep_ref = refs[:chunks], refs[chunks], refs[chunks + 1], refs[chunks + 2]
    me = info_ref[0]
    peer = jnp.bitwise_xor(me, 1)
    x = jnp.concatenate([x_ref[...] for x_ref in x_refs], axis=0) if chunks > 1 else x_refs[0][...]
    width = x.shape[1]
    for p in range(len(tables[0])):
        for device, out_ref in ((peer, send_ref), (me, keep_ref)):
            at = pl.multiple_of(block_at(device, p, tables) * width, width)
            part = jnp.dot(x, w_ref[:, pl.ds(at, width)], preferred_element_type=jnp.float32)
            out_ref[p] = part.astype(out_ref.dtype)


def tiles_kernel(tables, info_ref, segment_ref, *refs):
    down_hbm, up_hbm, down_send, up_send, down_keep, up_keep, code_ref = refs[:7]
    held_ref, sems = refs[7:]
    me = info_ref[0]
    peer = jnp.bitwise_xor(me, 1)
    width = down_keep.shape[2]
    rank = down_hbm.shape[1]
    copies = []
    for j in range(PICKED):
        for k, source in enumerate((down_hbm, up_hbm)):
            at = 2 * j + k
            copies.append(
                pltpu.make_async_copy(source.at[info_ref[1 + j]], held_ref.at[at], sems.at[at])
            )
            copies[-1].start()
    segment = segment_ref[...]
    code = jnp.zeros(segment.shape, jnp.int32)
    for s in range(info_ref.shape[0] - 1 - PICKED):
        code = jnp.where(segment == s, info_ref[1 + PICKED + s], code)
    code_ref[...] = code
    for j in range(PICKED):
        rows = slice(j * rank, (j + 1) * rank)
        for k, (send, keep) in enumerate(((down_send, down_keep), (up_send, up_keep))):
            copies[2 * j + k].wait()
            for p in range(len(tables[0])):
                for device, out in ((peer, send), (me, keep)):
                    at = pl.multiple_of(block_at(device, p, tables) * width, width)
                    out[p, rows, :] = held_ref[2 * j + k, :, pl.ds(at, width)]


def shrink_sums(x_ref, own_ref, peer_ref, first, own, peer):
    contract = (((1,), (1,)), ((), ()))
    for p in range(x_ref.shape[0]):
        x = x_ref[p]
        own = own + lax.dot_general(
            x, own_ref[first + p], contract, preferred_element_type=jnp.float32
        )
        peer = peer + lax.dot_general(
            x, peer_ref[first + p], contract, preferred_element_type=jnp.float32
        )
    return own, peer


def shrink_start_kernel(x_ref, own_ref, peer_ref, out_ref):
    zero = jnp.zeros(out_ref.shape[1:], jnp.float32)
    out_ref[0], out_ref[1] = shrink_sums(x_ref, own_ref, peer_ref, 0, zero, zero)


def shrink_kernel(code_ref, sums_ref, x_ref, own_ref, peer_ref, out_ref):
    rows, rank = out_ref.shape
    sums = shrink_sums(x_ref, own_ref, peer_ref, x_ref.shape[0], sums_ref[0], sums_ref[1])
    code = code_ref[...]
    total = jnp.zeros((rows, rank), jnp.float32)
    for place, part in enumerate(sums):
        for j in range(PICKED):
            value = part[:, j * rank : (j + 1) * rank]
            total = total + jnp.where(code == 1 + place * PICKED + j, value, 0.0)
    out_ref[...] = total


def expand_kernel(first, row, code_ref, mine_ref, got_ref, keep_ref, base_ref, own_ref, peer_ref, out_ref):
    positions, rows, _ = out_ref.shape
    half = (mine_ref[...] + got_ref[...]).astype(jnp.bfloat16)
    code = code_ref[...]
    picked = [
        jnp.where(code == 1 + j, half.astype(jnp.float32), 0.0).astype(jnp.bfloat16)
        for j in range(2 * PICKED)
    ]
    own = jnp.concatenate(picked[:PICKED], axis=1)
    peer = jnp.concatenate(picked[PICKED:], axis=1)
    for p in range(positions):
        at = first + p
        term = jnp.dot(own, own_ref[at], preferred_element_type=jnp.float32)
        term = term + jnp.dot(peer, peer_ref[at], preferred_element_type=jnp.float32)
        base = keep_ref[at, row : row + rows] + base_ref[at, row : row + rows].astype(jnp.float32)
        out_ref[p] = (base + ADAPTER_SCALE * term).astype(out_ref.dtype)


def after(values, *earlier):
    return lax.optimization_barrier((values, earlier))[0]


def smem():
    return pl.BlockSpec(memory_space=pltpu.SMEM)


def vmem():
    return pl.BlockSpec(memory_space=pltpu.VMEM)


def in_hbm(value):
    return pltpu.with_memory_space_constraint(value, pltpu.HBM)


def params(**more):
    return pltpu.CompilerParams(vmem_limit_bytes=VMEM_LIMIT, **more)


def owner_side(
    attention_output,
    output_weight,
    down_weight,
    up_weight,
    store_adapter_ids,
    segment_adapter,
    segment_rows,
):
    bf16, f32 = jnp.bfloat16, jnp.float32
    device_count = lax.axis_size("replica")
    me = lax.axis_index("replica")
    total_rows, width = attention_output.shape
    held, _, rank = down_weight.shape
    seg_count = segment_rows.shape[0]
    live_rows = total_rows - seg_count * (BLOCK - 1)
    step = live_rows // CHUNKS
    even_masks, odd_masks = stage_masks(device_count)
    tables = (position_masks(even_masks), position_masks(odd_masks))
    positions = len(tables[0])

    slot = slot_lookup(store_adapter_ids, segment_adapter)
    owner, local = slot // held, slot % held

    def picks(device):
        here = owner == device
        low = jnp.minimum(jnp.min(jnp.where(here, local, held)), held - 1)
        high = jnp.max(jnp.where(here, local, 0))
        return here, low, high

    own_here, own_low, own_high = picks(me)
    peer_here, peer_low, _ = picks(me ^ 1)
    place = jnp.where(own_here, jnp.where(local == own_low, 1, 2), 0)
    place = jnp.where(peer_here, PICKED + jnp.where(local == peer_low, 1, 2), place)
    info = jnp.concatenate([jnp.stack([me, own_low, own_high]), place]).astype(jnp.int32)

    hbm = pl.BlockSpec(memory_space=pltpu.HBM)
    *live, pick, segment = pl.pallas_call(
        lambda *refs: compact_kernel(CHUNKS, *refs),
        out_shape=[jax.ShapeDtypeStruct((step, width), bf16)] * CHUNKS
        + [
            jax.ShapeDtypeStruct((total_rows, live_rows), bf16),
            jax.ShapeDtypeStruct((live_rows, rank), jnp.int32),
        ],
        in_specs=[hbm, hbm],
        out_specs=[vmem()] * (CHUNKS + 2),
        scratch_shapes=[
            pltpu.SMEM(segment_rows.shape, jnp.int32),
            pltpu.VMEM(attention_output.shape, bf16),
            pltpu.SemaphoreType.DMA,
            pltpu.SemaphoreType.DMA,
        ],
        compiler_params=params(),
        name="compact_rows",
    )(in_hbm(segment_rows), in_hbm(attention_output))

    def cut_tiles(info):
        tile = jax.ShapeDtypeStruct((positions, PICKED * rank, width), bf16)
        return pl.pallas_call(
            lambda *refs: tiles_kernel(tables, *refs),
            out_shape=[tile] * 4 + [jax.ShapeDtypeStruct((live_rows, rank), jnp.int32)],
            in_specs=[smem(), vmem(), hbm, hbm],
            out_specs=[vmem()] * 5,
            scratch_shapes=[
                pltpu.VMEM((2 * PICKED, rank, down_weight.shape[1]), bf16),
                pltpu.SemaphoreType.DMA((2 * PICKED,)),
            ],
            compiler_params=params(),
            name="cut_tiles",
        )(
            info,
            segment,
            in_hbm(jnp.transpose(down_weight, (0, 2, 1))),
            in_hbm(jnp.transpose(up_weight, (0, 2, 1))),
        )

    def base_partials(info):
        return pl.pallas_call(
            lambda *refs: base_kernel(tables, CHUNKS, *refs),
            out_shape=[
                jax.ShapeDtypeStruct((positions, live_rows, width), bf16),
                jax.ShapeDtypeStruct((positions, live_rows, width), f32),
            ],
            in_specs=[smem()] + [vmem()] * (CHUNKS + 1),
            out_specs=[vmem()] * 2,
            compiler_params=params(),
            name="base_partials",
        )(info, *live, output_weight)

    def shrink_start(x):
        return pl.pallas_call(
            shrink_start_kernel,
            out_shape=jax.ShapeDtypeStruct((2, step, PICKED * rank), f32),
            in_specs=[vmem()] * 3,
            out_specs=vmem(),
            compiler_params=params(),
            name="shrink_start",
        )(x, down_own, down_peer)

    def shrink(i, sums, x):
        return pl.pallas_call(
            shrink_kernel,
            out_shape=jax.ShapeDtypeStruct((step, rank), f32),
            in_specs=[vmem()] * 5,
            out_specs=vmem(),
            compiler_params=params(),
            name="shrink",
        )(codes[i], sums, x, down_own, down_peer)

    def expand(i, part, dtype):
        return pl.pallas_call(
            lambda *refs: expand_kernel(part * half, i * step, *refs),
            out_shape=jax.ShapeDtypeStruct((half, step, width), dtype),
            in_specs=[vmem()] * 7,
            out_specs=vmem(),
            compiler_params=params(),
            name="expand",
        )(codes[i], mine[i], theirs[i], base_keep, base_got, up_own, up_peer)

    stages = list(zip(even_masks, odd_masks))
    cut_at, base_at = len(stages) - 2, len(stages) - 1
    gathered = [part[None] for part in live]
    for k, (mask_even, mask_odd) in enumerate(stages):
        got = [exchange(part, mask_even, mask_odd) for part in gathered]
        done = ()
        if k == base_at:
            base_send, base_keep = base_partials(after(info, gathered) if k else info)
            base_got = exchange(base_send, 1, 1)
            done = (base_send,)
        if k == cut_at:
            down_send, up_send, down_own, up_own, code = cut_tiles(after(info, gathered))
            down_peer = exchange(down_send, 1, 1)
            up_peer = exchange(up_send, 1, 1)
            done = (down_send,)
        if k < len(stages) - 1:
            gathered = [jnp.concatenate(pair, axis=0) for pair in zip(gathered, got)]
        if done:
            gathered = after(gathered, *done)

    half = positions // 2
    codes = [code[i * step : (i + 1) * step] for i in range(CHUNKS)]
    sums = [shrink_start(part) for part in gathered]
    mine, theirs, send = [], [], []
    for i in range(CHUNKS):
        last = got[i] if i == 0 else after(got[i], send[i - 1])
        mine.append(shrink(i, sums[i], last))
        theirs.append(exchange(mine[i], 1, 1))
        send.append(expand(i, 1, bf16))
    keep = [expand(i, 0, f32) for i in range(CHUNKS)]

    for k, (mask_even, mask_odd) in enumerate(reversed(stages)):
        if k:
            left = keep[0].shape[0] // 2
            sums = [a + b.astype(f32) for a, b in zip(keep, got)]
            keep = [value[:left] for value in sums]
            send = [value[left:].astype(bf16) for value in sums]
        got = [exchange(value, mask_even, mask_odd) for value in send]
    return pl.pallas_call(
        lambda *refs: spread_rows_kernel(CHUNKS, *refs),
        out_shape=jax.ShapeDtypeStruct((total_rows, width), bf16),
        in_specs=[vmem()] * (2 * CHUNKS + 1),
        out_specs=vmem(),
        compiler_params=params(),
        name="spread_rows",
    )(pick, *keep, *got)


def per_device(*arrays):
    width, features = arrays[0].shape[1], arrays[1].shape[1]
    if width % 128 == 0 and lax.axis_size("replica") >= 4:
        return owner_side(*arrays)
    return tile_side(*arrays)


def solution(mesh):
    in_specs = (
        P("parts", "replica"),
        P("replica", None),
        P(("parts", "replica"), None, None),
        P(("parts", "replica"), None, None),
        P("parts"),
        P("parts"),
        P("parts"),
    )
    out_specs = P("parts", "replica")
    return jax.shard_map(
        per_device, mesh=mesh, in_specs=in_specs, out_specs=out_specs, check_vma=False
    )
```

```python
import jax
import jax.numpy as jnp
from jax import lax
from jax.experimental import pallas as pl
from jax.experimental.pallas import tpu as pltpu
from jax.sharding import PartitionSpec as P

BLOCK = 4


ADAPTER_SCALE = 2.0

PICKED = 2

VMEM_LIMIT = 16 * 1024 * 1024


def segment_member(segment_rows, total_rows, block_rows):
    padded = (segment_rows + block_rows - 1) // block_rows * block_rows
    starts = jnp.cumsum(padded) - padded
    row_ids = jnp.arange(total_rows, dtype=jnp.int32)
    inside = (row_ids[:, None] >= starts[None, :]) & (
        row_ids[:, None] < (starts + segment_rows)[None, :]
    )
    return inside.astype(jnp.float32)


def slot_lookup(store_adapter_ids, segment_adapter):
    positions = jnp.arange(store_adapter_ids.shape[0], dtype=jnp.int32)
    equal = store_adapter_ids[None, :] == segment_adapter[:, None]
    return jnp.sum(jnp.where(equal, positions[None, :], 0), axis=1)


def tile_side(
    attention_output,
    output_weight,
    down_weight,
    up_weight,
    store_adapter_ids,
    segment_adapter,
    segment_rows,
):
    device_list = lax.axis_size("replica")
    total_rows, feature_columns = attention_output.shape
    holding_count, hidden_width, adapter_rank_size = down_weight.shape
    seg_count = segment_rows.shape[0]
    member = segment_member(segment_rows, total_rows, BLOCK)
    active_rows = jnp.sum(member, axis=1)
    slot_for_adapter = slot_lookup(store_adapter_ids, segment_adapter)
    partial_value = jnp.dot(attention_output, output_weight, preferred_element_type=jnp.float32)
    down_pieces = down_weight.reshape(
        holding_count, device_list, feature_columns, adapter_rank_size
    )
    up_pieces = up_weight.reshape(holding_count, device_list, feature_columns, adapter_rank_size)
    tile_pairs = jnp.concatenate([down_pieces, up_pieces], axis=3)
    arrived = lax.all_to_all(tile_pairs, "replica", split_axis=1, concat_axis=0, tiled=True)
    arrived = arrived.reshape(-1, feature_columns, 2 * adapter_rank_size)
    seg_tiles = arrived[slot_for_adapter]
    a_part = seg_tiles[:, :, :adapter_rank_size]
    b_part = seg_tiles[:, :, adapter_rank_size:]
    a_matrix = jnp.transpose(a_part, (1, 0, 2)).reshape(
        feature_columns, seg_count * adapter_rank_size
    )
    shrink_all = jnp.dot(attention_output, a_matrix, preferred_element_type=jnp.float32)
    shrink_all = shrink_all.reshape(total_rows, seg_count, adapter_rank_size)
    shrink_part = jnp.einsum("ps,psr->pr", member, shrink_all)
    base_column_block = lax.psum_scatter(partial_value, "replica", scatter_dimension=1, tiled=True)
    shrink = lax.psum(shrink_part, "replica")
    shrink_half = shrink.astype(jnp.bfloat16)
    spread = (member[:, :, None] * shrink_half.astype(jnp.float32)[:, None, :]).astype(jnp.bfloat16)
    spread = spread.reshape(total_rows, seg_count * adapter_rank_size)
    b_matrix = jnp.transpose(b_part, (0, 2, 1)).reshape(
        seg_count * adapter_rank_size, feature_columns
    )
    adapter_column_block = jnp.dot(spread, b_matrix, preferred_element_type=jnp.float32)
    mixed = active_rows[:, None] * (base_column_block + ADAPTER_SCALE * adapter_column_block)
    return mixed.astype(jnp.bfloat16)


def stage_masks(device_count):
    masks = []
    mask = device_count // 2
    while mask >= 2:
        masks.append(mask)
        mask //= 2
    other = list(masks)
    if len(other) >= 2:
        other[-1], other[-2] = other[-2], other[-1]
    return masks, other


def stage_groups(even, odd):
    pairs = list(zip(even, odd))
    groups = [pairs[:2]] + [[pair] for pair in pairs[2:]] if len(pairs) > 2 else [[p] for p in pairs]
    found = []
    for group in groups:
        masks = [(0, 0)]
        for even_mask, odd_mask in group:
            masks = masks + [(a ^ even_mask, b ^ odd_mask) for a, b in masks]
        found.append(masks[1:])
    return found


def chain_rows(live_rows):
    return live_rows - live_rows // 2, live_rows // 2


def position_masks(masks):
    found = [0]
    for mask in masks:
        found = found + [value ^ mask for value in found]
    return found


def exchange(value, mask_even, mask_odd):
    count = lax.axis_size("replica")
    pairs = [(i, i ^ (mask_odd if i & 1 else mask_even)) for i in range(count)]
    return lax.ppermute(value, "replica", pairs)


def block_at(device, position, tables):
    even, odd = tables[0][position], tables[1][position]
    if even == odd:
        return jnp.bitwise_xor(device, even)
    return jnp.bitwise_xor(device, jnp.where(jnp.bitwise_and(device, 1) == 0, even, odd))


def padded_row(live_row, rows_ref):
    place = live_row
    end = jnp.int32(0)
    for s in range(rows_ref.shape[0]):
        count = rows_ref[s]
        gap = (BLOCK - count % BLOCK) % BLOCK
        end = end + count
        place = place + jnp.where(live_row >= end, gap, 0)
    return place


def compact_kernel(rows_hbm, x_hbm, wanted_hbm, store_hbm, *refs):
    out_ref, pick_ref, code_ref, slot_ref, rows_ref, x_ref, wanted_ref, store_ref, sems = refs
    rows_copy, x_copy, wanted_copy, store_copy = (
        pltpu.make_async_copy(source, target, sems.at[i])
        for i, (source, target) in enumerate(
            (
                (rows_hbm, rows_ref),
                (x_hbm, x_ref),
                (wanted_hbm, wanted_ref),
                (store_hbm, store_ref),
            )
        )
    )
    for copy in (rows_copy, x_copy, wanted_copy, store_copy):
        copy.start()
    rows_copy.wait()
    shape = (out_ref.shape[0], x_ref.shape[0])
    live_row = lax.broadcasted_iota(jnp.int32, shape, 0)
    layout_row = lax.broadcasted_iota(jnp.int32, shape, 1)
    pick = jnp.where(padded_row(live_row, rows_ref) == layout_row, 1.0, 0.0).astype(jnp.bfloat16)
    x_copy.wait()
    rows = jnp.dot(pick, x_ref[...], preferred_element_type=jnp.float32)
    out_ref[...] = rows.astype(jnp.bfloat16)
    shape = pick_ref.shape
    live_row = lax.broadcasted_iota(jnp.int32, shape, 1)
    layout_row = lax.broadcasted_iota(jnp.int32, shape, 0)
    back = padded_row(live_row, rows_ref) == layout_row
    pick_ref[...] = jnp.where(back, 1.0, 0.0).astype(jnp.bfloat16)
    live_row = lax.broadcasted_iota(jnp.int32, code_ref.shape, 0)
    segment = jnp.zeros(code_ref.shape, jnp.int32)
    end = jnp.int32(0)
    for s in range(rows_ref.shape[0] - 1):
        end = end + rows_ref[s]
        segment = segment + jnp.where(live_row >= end, 1, 0)
    code_ref[...] = segment
    wanted_copy.wait()
    store_copy.wait()
    shape = (wanted_ref.shape[0], store_ref.shape[1])
    row = lax.broadcasted_iota(jnp.int32, shape, 0)
    lane = lax.broadcasted_iota(jnp.int32, shape, 1)
    wanted = jnp.zeros(shape, jnp.int32)
    for s in range(shape[0]):
        wanted = jnp.where(row == s, wanted_ref[s], wanted)
    found = jnp.where(store_ref[...] == wanted, lane, 0).astype(jnp.float32)
    slot_ref[...] = jnp.broadcast_to(jnp.sum(found, axis=1, keepdims=True), slot_ref.shape)


def spread_rows_kernel(chains, pick_ref, *refs):
    keep_refs, got_refs, out_ref = refs[:chains], refs[chains:-1], refs[-1]
    each = len(got_refs) // chains
    live = []
    for i, keep_ref in enumerate(keep_refs):
        total = keep_ref[0]
        for got_ref in got_refs[i * each : (i + 1) * each]:
            total = total + got_ref[0].astype(jnp.float32)
        live.append(total.astype(jnp.bfloat16))
    mixed = live[0] if chains == 1 else jnp.concatenate(live, axis=0)
    out = jnp.dot(pick_ref[...], mixed, preferred_element_type=jnp.float32)
    out_ref[...] = out.astype(jnp.bfloat16)


def find_kernel(held, me_ref, slot_ref, segment_ref, info_ref, code_ref):
    me = me_ref[0]
    segs = slot_ref.shape[0]
    slot = slot_ref[:, :1]
    place = jnp.zeros((segs, 1), jnp.float32)
    for first, device in ((0, me), (PICKED, jnp.bitwise_xor(me, 1))):
        local = slot - (device * held).astype(jnp.float32)
        here = (local >= 0.0) & (local < held)
        low = jnp.minimum(jnp.min(jnp.where(here, local, float(held))), held - 1.0)
        place = jnp.where(here, jnp.where(local == low, first + 1.0, first + 2.0), place)
        if first == 0:
            info_ref[0] = me
            info_ref[1] = low.astype(jnp.int32)
            info_ref[2] = jnp.max(jnp.where(here, local, 0.0)).astype(jnp.int32)
    segment = segment_ref[...]
    code = jnp.zeros(segment.shape, jnp.float32)
    for s in range(segs):
        code = jnp.where(segment == s, place[s : s + 1, :], code)
    code_ref[...] = code


def base_kernel(tables, me_ref, x_ref, w_hbm, send_ref, keep_ref, w_ref, sems):
    me = me_ref[0]
    peer = jnp.bitwise_xor(me, 1)
    parts, group_width = w_ref.shape[0], w_ref.shape[2]
    width = x_ref.shape[1]
    group = group_width // width
    copies = []
    for g in range(parts):
        at = pl.multiple_of(jnp.bitwise_xor(me // group, g) * group_width, group_width)
        copies.append(
            pltpu.make_async_copy(w_hbm.at[:, pl.ds(at, group_width)], w_ref.at[g], sems.at[g])
        )
        copies[-1].start()
    x = x_ref[...]
    for g in range(parts):
        copies[g].wait()
        for p in range(len(tables[0])):
            if tables[0][p] // group != g:
                continue
            for device, out_ref in ((peer, send_ref), (me, keep_ref)):
                at = pl.multiple_of(block_at(device, p, tables) % group * width, width)
                part = jnp.dot(
                    x, w_ref[g, :, pl.ds(at, width)], preferred_element_type=jnp.float32
                )
                out_ref[p] = part.astype(out_ref.dtype)


def tiles_kernel(tables, info_ref, *refs):
    stores, outs, held_ref, sems = refs[:2], refs[2:6], refs[6], refs[7]
    me = info_ref[0]
    peer = jnp.bitwise_xor(me, 1)
    width = outs[0].shape[2]
    rank = stores[0].shape[1]
    copies = []
    for k, store in enumerate(stores):
        for j in range(PICKED):
            at = PICKED * k + j
            copies.append(
                pltpu.make_async_copy(store.at[info_ref[1 + j]], held_ref.at[at], sems.at[at])
            )
            copies[-1].start()
    for at, copy in enumerate(copies):
        copy.wait()
        k, j = at // PICKED, at % PICKED
        for p in range(len(tables[0])):
            for device, out in ((peer, outs[2 * k]), (me, outs[2 * k + 1])):
                lane = pl.multiple_of(block_at(device, p, tables) * width, width)
                out[p, j * rank : (j + 1) * rank, :] = held_ref[at, :, pl.ds(lane, width)]


def shrink_sums(places, x_ref, own_ref, peer_ref, own, peer):
    contract = (((1,), (1,)), ((), ()))
    for p, at in enumerate(places):
        x = x_ref[p]
        own = own + lax.dot_general(x, own_ref[at], contract, preferred_element_type=jnp.float32)
        peer = peer + lax.dot_general(x, peer_ref[at], contract, preferred_element_type=jnp.float32)
    return own, peer


def shrink_start_kernel(places, x_ref, own_ref, peer_ref, out_ref):
    zero = jnp.zeros(out_ref.shape[1:], jnp.float32)
    out_ref[0], out_ref[1] = shrink_sums(places, x_ref, own_ref, peer_ref, zero, zero)


def shrink_kernel(row, places, code_ref, sums_ref, x_ref, own_ref, peer_ref, out_ref):
    rows, rank = out_ref.shape
    sums = shrink_sums(places, x_ref, own_ref, peer_ref, sums_ref[0], sums_ref[1])
    code = code_ref[row : row + rows, :]
    total = jnp.zeros((rows, rank), jnp.float32)
    for place, part in enumerate(sums):
        for j in range(PICKED):
            value = part[:, j * rank : (j + 1) * rank]
            total = total + jnp.where(code == 1 + place * PICKED + j, value, 0.0)
    out_ref[...] = total


def expand_kernel(
    row, places, code_ref, mine_ref, got_ref, keep_ref, base_ref, own_ref, peer_ref, out_ref
):
    rows = out_ref.shape[1]
    half = (mine_ref[...] + got_ref[...]).astype(jnp.bfloat16)
    code = code_ref[row : row + rows, :]
    picked = [
        jnp.where(code == 1 + j, half.astype(jnp.float32), 0.0).astype(jnp.bfloat16)
        for j in range(2 * PICKED)
    ]
    own = jnp.concatenate(picked[:PICKED], axis=1)
    peer = jnp.concatenate(picked[PICKED:], axis=1)
    for p, at in enumerate(places):
        term = jnp.dot(own, own_ref[at], preferred_element_type=jnp.float32)
        term = term + jnp.dot(peer, peer_ref[at], preferred_element_type=jnp.float32)
        base = keep_ref[at, row : row + rows] + base_ref[at, row : row + rows].astype(jnp.float32)
        out_ref[p] = (base + ADAPTER_SCALE * term).astype(out_ref.dtype)


def after(values, *earlier):
    return lax.optimization_barrier((values, earlier))[0]


def smem():
    return pl.BlockSpec(memory_space=pltpu.SMEM)


def vmem():
    return pl.BlockSpec(memory_space=pltpu.VMEM)


def in_hbm(value):
    return pltpu.with_memory_space_constraint(value, pltpu.HBM)


def params(**more):
    return pltpu.CompilerParams(vmem_limit_bytes=VMEM_LIMIT, **more)


def owner_side(
    attention_output,
    output_weight,
    down_weight,
    up_weight,
    store_adapter_ids,
    segment_adapter,
    segment_rows,
):
    bf16, f32 = jnp.bfloat16, jnp.float32
    device_count = lax.axis_size("replica")
    me = lax.axis_index("replica")
    total_rows, width = attention_output.shape
    held, _, rank = down_weight.shape
    seg_count = segment_rows.shape[0]
    live_rows = total_rows - seg_count * (BLOCK - 1)
    sizes = chain_rows(live_rows)
    chains = len(sizes)
    starts = [sum(sizes[:i]) for i in range(chains)]
    even_masks, odd_masks = stage_masks(device_count)
    tables = (position_masks(even_masks), position_masks(odd_masks))
    positions = len(tables[0])
    half = positions // 2
    groups = stage_groups(even_masks, odd_masks)

    me = jnp.reshape(me, (1,))

    hbm = pl.BlockSpec(memory_space=pltpu.HBM)
    live, pick, segment, slots = pl.pallas_call(
        compact_kernel,
        out_shape=[
            jax.ShapeDtypeStruct((live_rows, width), bf16),
            jax.ShapeDtypeStruct((total_rows, live_rows), bf16),
            jax.ShapeDtypeStruct((live_rows, rank), jnp.int32),
            jax.ShapeDtypeStruct((seg_count, 128), f32),
        ],
        in_specs=[hbm] * 4,
        out_specs=[vmem()] * 4,
        scratch_shapes=[
            pltpu.SMEM(segment_rows.shape, jnp.int32),
            pltpu.VMEM(attention_output.shape, bf16),
            pltpu.SMEM(segment_adapter.shape, jnp.int32),
            pltpu.VMEM((1, store_adapter_ids.shape[0]), jnp.int32),
            pltpu.SemaphoreType.DMA((4,)),
        ],
        compiler_params=params(),
        name="compact_rows",
    )(
        in_hbm(segment_rows),
        in_hbm(attention_output),
        in_hbm(segment_adapter),
        in_hbm(jnp.reshape(store_adapter_ids, (1, -1))),
    )

    info, code = pl.pallas_call(
        lambda *refs: find_kernel(held, *refs),
        out_shape=[
            jax.ShapeDtypeStruct((1 + PICKED,), jnp.int32),
            jax.ShapeDtypeStruct((live_rows, rank), f32),
        ],
        in_specs=[smem(), vmem(), vmem()],
        out_specs=[smem(), vmem()],
        compiler_params=params(),
        name="find_adapters",
    )(me, slots, segment)

    def cut_tiles(info):
        return pl.pallas_call(
            lambda *refs: tiles_kernel(tables, *refs),
            out_shape=[jax.ShapeDtypeStruct((positions, PICKED * rank, width), bf16)] * 4,
            in_specs=[smem(), hbm, hbm],
            out_specs=[vmem()] * 4,
            scratch_shapes=[
                pltpu.VMEM((2 * PICKED, rank, down_weight.shape[1]), bf16),
                pltpu.SemaphoreType.DMA((2 * PICKED,)),
            ],
            compiler_params=params(),
            name="cut_tiles",
        )(
            info,
            in_hbm(jnp.transpose(down_weight, (0, 2, 1))),
            in_hbm(jnp.transpose(up_weight, (0, 2, 1))),
        )

    def base_partials(me):
        parts = 4
        return pl.pallas_call(
            lambda *refs: base_kernel(tables, *refs),
            out_shape=[
                jax.ShapeDtypeStruct((positions, live_rows, width), bf16),
                jax.ShapeDtypeStruct((positions, live_rows, width), f32),
            ],
            in_specs=[smem(), vmem(), hbm],
            out_specs=[vmem()] * 2,
            scratch_shapes=[
                pltpu.VMEM((parts, width, output_weight.shape[1] // parts), bf16),
                pltpu.SemaphoreType.DMA((parts,)),
            ],
            compiler_params=params(),
            name="base_partials",
        )(me, live, in_hbm(output_weight))

    def shrink_start(i, x):
        return pl.pallas_call(
            lambda *refs: shrink_start_kernel(range(half), *refs),
            out_shape=jax.ShapeDtypeStruct((2, sizes[i], PICKED * rank), f32),
            in_specs=[vmem()] * 3,
            out_specs=vmem(),
            compiler_params=params(),
            name="shrink_start",
        )(x, down_own, down_peer)

    def shrink(i, sums, x):
        return pl.pallas_call(
            lambda *refs: shrink_kernel(starts[i], range(half, positions), *refs),
            out_shape=jax.ShapeDtypeStruct((sizes[i], rank), f32),
            in_specs=[vmem()] * 5,
            out_specs=vmem(),
            compiler_params=params(),
            name="shrink",
        )(code, sums, x, down_own, down_peer)

    def expand(i, part, dtype):
        return pl.pallas_call(
            lambda *refs: expand_kernel(
                starts[i], range(part * half, (part + 1) * half), *refs
            ),
            out_shape=jax.ShapeDtypeStruct((half, sizes[i], width), dtype),
            in_specs=[vmem()] * 7,
            out_specs=vmem(),
            compiler_params=params(),
            name="expand",
        )(code, mine[i], theirs[i], base_keep, base_got, up_own, up_peer)

    def swap(parts, masks):
        return [exchange(part, *mask) for part, mask in zip(parts, masks)]

    stages = len(groups)
    cut_at = max(stages - 2, 0)
    gathered = live[None]
    for k, masks in enumerate(groups):
        before = gathered
        if k < stages - 1:
            got = swap([gathered] * len(masks), masks)
            gathered = jnp.concatenate([gathered, *got], axis=0)
        else:
            gathered = [gathered[:, a : a + n] for a, n in zip(starts, sizes)]
            got = [exchange(part, *masks[0]) for part in gathered]
        if k == 0:
            base_send, base_keep = base_partials(me)
            gathered, base_send = after((gathered, base_send))
            base_got = exchange(base_send, 1, 1)
        if k == cut_at:
            down_send, down_own, up_send, up_own = cut_tiles(after(info, before))
            gathered, down_send, up_send = after((gathered, down_send, up_send))
            down_peer = exchange(down_send, 1, 1)
            up_peer = exchange(up_send, 1, 1)

    sums = [shrink_start(i, part) for i, part in enumerate(gathered)]

    mine, theirs, send = [None] * chains, [None] * chains, [None] * chains
    for i in range(chains):
        last = got[i] if i == 0 else after(got[i], send[i - 1])
        mine[i] = shrink(i, sums[i], last)
        theirs[i] = exchange(mine[i], 1, 1)
        send[i] = expand(i, 1, bf16)
    keep = [expand(i, 0, f32) for i in range(chains)]

    send = [[value] for value in send]
    for k, masks in reversed(list(enumerate(groups))):
        if k < stages - 1:
            total = [a + sum(part.astype(f32) for part in b) for a, b in zip(keep, got)]
            if k == 0:
                total = [jnp.concatenate(total, axis=1)]
            left = total[0].shape[0] // (len(masks) + 1)
            keep = [value[:left] for value in total]
            send = [
                [value[(j + 1) * left : (j + 2) * left].astype(bf16) for j in range(len(masks))]
                for value in total
            ]
        got = [swap(parts, masks) for parts in send]
    return pl.pallas_call(
        lambda *refs: spread_rows_kernel(len(keep), *refs),
        out_shape=jax.ShapeDtypeStruct((total_rows, width), bf16),
        in_specs=[vmem()] * (1 + len(keep) * (1 + len(groups[0]))),
        out_specs=vmem(),
        compiler_params=params(),
        name="spread_rows",
    )(pick, *keep, *[part for parts in got for part in parts])


def per_device(*arrays):
    width, features = arrays[0].shape[1], arrays[1].shape[1]
    if width % 128 == 0 and lax.axis_size("replica") >= 4:
        return owner_side(*arrays)
    return tile_side(*arrays)


def solution(mesh):
    in_specs = (
        P("parts", "replica"),
        P("replica", None),
        P(("parts", "replica"), None, None),
        P(("parts", "replica"), None, None),
        P("parts"),
        P("parts"),
        P("parts"),
    )
    out_specs = P("parts", "replica")
    return jax.shard_map(
        per_device, mesh=mesh, in_specs=in_specs, out_specs=out_specs, check_vma=False
    )
```

```python
import jax
import jax.numpy as jnp
from jax import lax
from jax.experimental import pallas as pl
from jax.experimental.pallas import tpu as pltpu
from jax.sharding import PartitionSpec as P

BLOCK = 4


ADAPTER_SCALE = 2.0

PICKED = 2

VMEM_LIMIT = 16 * 1024 * 1024


def segment_member(segment_rows, total_rows, block_rows):
    padded = (segment_rows + block_rows - 1) // block_rows * block_rows
    starts = jnp.cumsum(padded) - padded
    row_ids = jnp.arange(total_rows, dtype=jnp.int32)
    inside = (row_ids[:, None] >= starts[None, :]) & (
        row_ids[:, None] < (starts + segment_rows)[None, :]
    )
    return inside.astype(jnp.float32)


def slot_lookup(store_adapter_ids, segment_adapter):
    positions = jnp.arange(store_adapter_ids.shape[0], dtype=jnp.int32)
    equal = store_adapter_ids[None, :] == segment_adapter[:, None]
    return jnp.sum(jnp.where(equal, positions[None, :], 0), axis=1)


def tile_side(
    attention_output,
    output_weight,
    down_weight,
    up_weight,
    store_adapter_ids,
    segment_adapter,
    segment_rows,
):
    device_list = lax.axis_size("replica")
    total_rows, feature_columns = attention_output.shape
    holding_count, hidden_width, adapter_rank_size = down_weight.shape
    seg_count = segment_rows.shape[0]
    member = segment_member(segment_rows, total_rows, BLOCK)
    active_rows = jnp.sum(member, axis=1)
    slot_for_adapter = slot_lookup(store_adapter_ids, segment_adapter)
    partial_value = jnp.dot(attention_output, output_weight, preferred_element_type=jnp.float32)
    down_pieces = down_weight.reshape(
        holding_count, device_list, feature_columns, adapter_rank_size
    )
    up_pieces = up_weight.reshape(holding_count, device_list, feature_columns, adapter_rank_size)
    tile_pairs = jnp.concatenate([down_pieces, up_pieces], axis=3)
    arrived = lax.all_to_all(tile_pairs, "replica", split_axis=1, concat_axis=0, tiled=True)
    arrived = arrived.reshape(-1, feature_columns, 2 * adapter_rank_size)
    seg_tiles = arrived[slot_for_adapter]
    a_part = seg_tiles[:, :, :adapter_rank_size]
    b_part = seg_tiles[:, :, adapter_rank_size:]
    a_matrix = jnp.transpose(a_part, (1, 0, 2)).reshape(
        feature_columns, seg_count * adapter_rank_size
    )
    shrink_all = jnp.dot(attention_output, a_matrix, preferred_element_type=jnp.float32)
    shrink_all = shrink_all.reshape(total_rows, seg_count, adapter_rank_size)
    shrink_part = jnp.einsum("ps,psr->pr", member, shrink_all)
    base_column_block = lax.psum_scatter(partial_value, "replica", scatter_dimension=1, tiled=True)
    shrink = lax.psum(shrink_part, "replica")
    shrink_half = shrink.astype(jnp.bfloat16)
    spread = (member[:, :, None] * shrink_half.astype(jnp.float32)[:, None, :]).astype(jnp.bfloat16)
    spread = spread.reshape(total_rows, seg_count * adapter_rank_size)
    b_matrix = jnp.transpose(b_part, (0, 2, 1)).reshape(
        seg_count * adapter_rank_size, feature_columns
    )
    adapter_column_block = jnp.dot(spread, b_matrix, preferred_element_type=jnp.float32)
    mixed = active_rows[:, None] * (base_column_block + ADAPTER_SCALE * adapter_column_block)
    return mixed.astype(jnp.bfloat16)


def stage_masks(device_count):
    masks = []
    mask = device_count // 2
    while mask >= 2:
        masks.append(mask)
        mask //= 2
    other = list(masks)
    if len(other) >= 2:
        other[-1], other[-2] = other[-2], other[-1]
    return masks, other


def stage_groups(even, odd):
    pairs = list(zip(even, odd))
    groups = [pairs[:2]] + [[pair] for pair in pairs[2:]] if len(pairs) > 2 else [[p] for p in pairs]
    found = []
    for group in groups:
        masks = [(0, 0)]
        for even_mask, odd_mask in group:
            masks = masks + [(a ^ even_mask, b ^ odd_mask) for a, b in masks]
        found.append(masks[1:])
    return found


def chain_rows(live_rows):
    return live_rows - live_rows // 2, live_rows // 2


def position_masks(masks):
    found = [0]
    for mask in masks:
        found = found + [value ^ mask for value in found]
    return found


def exchange(value, mask_even, mask_odd):
    count = lax.axis_size("replica")
    pairs = [(i, i ^ (mask_odd if i & 1 else mask_even)) for i in range(count)]
    return lax.ppermute(value, "replica", pairs)


def block_at(device, position, tables):
    even, odd = tables[0][position], tables[1][position]
    if even == odd:
        return jnp.bitwise_xor(device, even)
    return jnp.bitwise_xor(device, jnp.where(jnp.bitwise_and(device, 1) == 0, even, odd))


def padded_row(live_row, rows_ref):
    place = live_row
    end = jnp.int32(0)
    for s in range(rows_ref.shape[0]):
        count = rows_ref[s]
        gap = (BLOCK - count % BLOCK) % BLOCK
        end = end + count
        place = place + jnp.where(live_row >= end, gap, 0)
    return place


def compact_kernel(rows_hbm, x_hbm, wanted_hbm, store_hbm, *refs):
    out_ref, pick_ref, code_ref, slot_ref, rows_ref, x_ref, wanted_ref, store_ref, sems = refs
    rows_copy, x_copy, wanted_copy, store_copy = (
        pltpu.make_async_copy(source, target, sems.at[i])
        for i, (source, target) in enumerate(
            (
                (rows_hbm, rows_ref),
                (x_hbm, x_ref),
                (wanted_hbm, wanted_ref),
                (store_hbm, store_ref),
            )
        )
    )
    for copy in (rows_copy, x_copy, wanted_copy, store_copy):
        copy.start()
    rows_copy.wait()
    shape = (out_ref.shape[0], x_ref.shape[0])
    live_row = lax.broadcasted_iota(jnp.int32, shape, 0)
    layout_row = lax.broadcasted_iota(jnp.int32, shape, 1)
    pick = jnp.where(padded_row(live_row, rows_ref) == layout_row, 1.0, 0.0).astype(jnp.bfloat16)
    x_copy.wait()
    rows = jnp.dot(pick, x_ref[...], preferred_element_type=jnp.float32)
    out_ref[...] = rows.astype(jnp.bfloat16)
    shape = pick_ref.shape
    live_row = lax.broadcasted_iota(jnp.int32, shape, 1)
    layout_row = lax.broadcasted_iota(jnp.int32, shape, 0)
    back = padded_row(live_row, rows_ref) == layout_row
    pick_ref[...] = jnp.where(back, 1.0, 0.0).astype(jnp.bfloat16)
    live_row = lax.broadcasted_iota(jnp.int32, code_ref.shape, 0)
    segment = jnp.zeros(code_ref.shape, jnp.int32)
    end = jnp.int32(0)
    for s in range(rows_ref.shape[0] - 1):
        end = end + rows_ref[s]
        segment = segment + jnp.where(live_row >= end, 1, 0)
    code_ref[...] = segment
    wanted_copy.wait()
    store_copy.wait()
    shape = (wanted_ref.shape[0], store_ref.shape[1])
    row = lax.broadcasted_iota(jnp.int32, shape, 0)
    lane = lax.broadcasted_iota(jnp.int32, shape, 1)
    wanted = jnp.zeros(shape, jnp.int32)
    for s in range(shape[0]):
        wanted = jnp.where(row == s, wanted_ref[s], wanted)
    found = jnp.where(store_ref[...] == wanted, lane, 0).astype(jnp.float32)
    slot_ref[...] = jnp.broadcast_to(jnp.sum(found, axis=1, keepdims=True), slot_ref.shape)


def spread_rows_kernel(chains, pick_ref, *refs):
    keep_refs, got_refs, out_ref = refs[:chains], refs[chains:-1], refs[-1]
    each = len(got_refs) // chains
    live = []
    for i, keep_ref in enumerate(keep_refs):
        total = keep_ref[0]
        for got_ref in got_refs[i * each : (i + 1) * each]:
            total = total + got_ref[0].astype(jnp.float32)
        live.append(total.astype(jnp.bfloat16))
    mixed = live[0] if chains == 1 else jnp.concatenate(live, axis=0)
    out = jnp.dot(pick_ref[...], mixed, preferred_element_type=jnp.float32)
    out_ref[...] = out.astype(jnp.bfloat16)


def find_kernel(held, me_ref, slot_ref, segment_ref, info_ref, code_ref):
    me = me_ref[0]
    segs = slot_ref.shape[0]
    slot = slot_ref[:, :1]
    place = jnp.zeros((segs, 1), jnp.float32)
    for first, device in ((0, me), (PICKED, jnp.bitwise_xor(me, 1))):
        local = slot - (device * held).astype(jnp.float32)
        here = (local >= 0.0) & (local < held)
        low = jnp.minimum(jnp.min(jnp.where(here, local, float(held))), held - 1.0)
        place = jnp.where(here, jnp.where(local == low, first + 1.0, first + 2.0), place)
        if first == 0:
            info_ref[0] = me
            info_ref[1] = low.astype(jnp.int32)
            info_ref[2] = jnp.max(jnp.where(here, local, 0.0)).astype(jnp.int32)
    segment = segment_ref[...]
    code = jnp.zeros(segment.shape, jnp.float32)
    for s in range(segs):
        code = jnp.where(segment == s, place[s : s + 1, :], code)
    code_ref[...] = code


def base_kernel(tables, me_ref, x_ref, w_hbm, send_ref, keep_ref, w_ref, sems):
    me = me_ref[0]
    peer = jnp.bitwise_xor(me, 1)
    parts, group_width = w_ref.shape[0], w_ref.shape[2]
    width = x_ref.shape[1]
    group = group_width // width
    copies = []
    for g in range(parts):
        at = pl.multiple_of(jnp.bitwise_xor(me // group, g) * group_width, group_width)
        copies.append(
            pltpu.make_async_copy(w_hbm.at[:, pl.ds(at, group_width)], w_ref.at[g], sems.at[g])
        )
        copies[-1].start()
    x = x_ref[...]
    for g in range(parts):
        copies[g].wait()
        for p in range(len(tables[0])):
            if tables[0][p] // group != g:
                continue
            for device, out_ref in ((peer, send_ref), (me, keep_ref)):
                at = pl.multiple_of(block_at(device, p, tables) % group * width, width)
                part = jnp.dot(
                    x, w_ref[g, :, pl.ds(at, width)], preferred_element_type=jnp.float32
                )
                out_ref[p] = part.astype(out_ref.dtype)


def tiles_kernel(tables, info_ref, *refs):
    stores, outs, held_ref, sems = refs[:2], refs[2:6], refs[6], refs[7]
    me = info_ref[0]
    peer = jnp.bitwise_xor(me, 1)
    width = outs[0].shape[2]
    rank = stores[0].shape[1]
    copies = []
    for k, store in enumerate(stores):
        for j in range(PICKED):
            at = PICKED * k + j
            copies.append(
                pltpu.make_async_copy(store.at[info_ref[1 + j]], held_ref.at[at], sems.at[at])
            )
            copies[-1].start()
    for at, copy in enumerate(copies):
        copy.wait()
        k, j = at // PICKED, at % PICKED
        for p in range(len(tables[0])):
            for device, out in ((peer, outs[2 * k]), (me, outs[2 * k + 1])):
                lane = pl.multiple_of(block_at(device, p, tables) * width, width)
                out[p, j * rank : (j + 1) * rank, :] = held_ref[at, :, pl.ds(lane, width)]


def shrink_sums(places, x_ref, own_ref, peer_ref, own, peer):
    contract = (((1,), (1,)), ((), ()))
    for p, at in enumerate(places):
        x = x_ref[p]
        own = own + lax.dot_general(x, own_ref[at], contract, preferred_element_type=jnp.float32)
        peer = peer + lax.dot_general(x, peer_ref[at], contract, preferred_element_type=jnp.float32)
    return own, peer


def shrink_start_kernel(places, x_ref, own_ref, peer_ref, out_ref):
    zero = jnp.zeros(out_ref.shape[1:], jnp.float32)
    out_ref[0], out_ref[1] = shrink_sums(places, x_ref, own_ref, peer_ref, zero, zero)


def shrink_kernel(row, places, code_ref, sums_ref, x_ref, own_ref, peer_ref, out_ref):
    rows, rank = out_ref.shape
    sums = shrink_sums(places, x_ref, own_ref, peer_ref, sums_ref[0], sums_ref[1])
    code = code_ref[row : row + rows, :]
    total = jnp.zeros((rows, rank), jnp.float32)
    for place, part in enumerate(sums):
        for j in range(PICKED):
            value = part[:, j * rank : (j + 1) * rank]
            total = total + jnp.where(code == 1 + place * PICKED + j, value, 0.0)
    out_ref[...] = total


def expand_kernel(
    row, places, code_ref, mine_ref, got_ref, keep_ref, base_ref, own_ref, peer_ref, out_ref
):
    rows = out_ref.shape[1]
    half = (mine_ref[...] + got_ref[...]).astype(jnp.bfloat16)
    code = code_ref[row : row + rows, :]
    picked = [
        jnp.where(code == 1 + j, half.astype(jnp.float32), 0.0).astype(jnp.bfloat16)
        for j in range(2 * PICKED)
    ]
    own = jnp.concatenate(picked[:PICKED], axis=1)
    peer = jnp.concatenate(picked[PICKED:], axis=1)
    for p, at in enumerate(places):
        term = jnp.dot(own, own_ref[at], preferred_element_type=jnp.float32)
        term = term + jnp.dot(peer, peer_ref[at], preferred_element_type=jnp.float32)
        base = keep_ref[at, row : row + rows] + base_ref[at, row : row + rows].astype(jnp.float32)
        out_ref[p] = (base + ADAPTER_SCALE * term).astype(out_ref.dtype)


def after(values, *earlier):
    return lax.optimization_barrier((values, earlier))[0]


def smem():
    return pl.BlockSpec(memory_space=pltpu.SMEM)


def vmem():
    return pl.BlockSpec(memory_space=pltpu.VMEM)


def in_hbm(value):
    return pltpu.with_memory_space_constraint(value, pltpu.HBM)


def params(**more):
    return pltpu.CompilerParams(vmem_limit_bytes=VMEM_LIMIT, **more)


def owner_side(
    attention_output,
    output_weight,
    down_weight,
    up_weight,
    store_adapter_ids,
    segment_adapter,
    segment_rows,
):
    bf16, f32 = jnp.bfloat16, jnp.float32
    device_count = lax.axis_size("replica")
    me = lax.axis_index("replica")
    total_rows, width = attention_output.shape
    held, _, rank = down_weight.shape
    seg_count = segment_rows.shape[0]
    live_rows = total_rows - seg_count * (BLOCK - 1)
    sizes = chain_rows(live_rows)
    chains = len(sizes)
    starts = [sum(sizes[:i]) for i in range(chains)]
    even_masks, odd_masks = stage_masks(device_count)
    tables = (position_masks(even_masks), position_masks(odd_masks))
    positions = len(tables[0])
    half = positions // 2
    groups = stage_groups(even_masks, odd_masks)

    me = jnp.reshape(me, (1,))

    hbm = pl.BlockSpec(memory_space=pltpu.HBM)
    live, pick, segment, slots = pl.pallas_call(
        compact_kernel,
        out_shape=[
            jax.ShapeDtypeStruct((live_rows, width), bf16),
            jax.ShapeDtypeStruct((total_rows, live_rows), bf16),
            jax.ShapeDtypeStruct((live_rows, rank), jnp.int32),
            jax.ShapeDtypeStruct((seg_count, 128), f32),
        ],
        in_specs=[hbm] * 4,
        out_specs=[vmem()] * 4,
        scratch_shapes=[
            pltpu.SMEM(segment_rows.shape, jnp.int32),
            pltpu.VMEM(attention_output.shape, bf16),
            pltpu.SMEM(segment_adapter.shape, jnp.int32),
            pltpu.VMEM((1, store_adapter_ids.shape[0]), jnp.int32),
            pltpu.SemaphoreType.DMA((4,)),
        ],
        compiler_params=params(),
        name="compact_rows",
    )(
        in_hbm(segment_rows),
        in_hbm(attention_output),
        in_hbm(segment_adapter),
        in_hbm(jnp.reshape(store_adapter_ids, (1, -1))),
    )

    info, code = pl.pallas_call(
        lambda *refs: find_kernel(held, *refs),
        out_shape=[
            jax.ShapeDtypeStruct((1 + PICKED,), jnp.int32),
            jax.ShapeDtypeStruct((live_rows, rank), f32),
        ],
        in_specs=[smem(), vmem(), vmem()],
        out_specs=[smem(), vmem()],
        compiler_params=params(),
        name="find_adapters",
    )(me, slots, segment)

    def cut_tiles(info):
        return pl.pallas_call(
            lambda *refs: tiles_kernel(tables, *refs),
            out_shape=[jax.ShapeDtypeStruct((positions, PICKED * rank, width), bf16)] * 4,
            in_specs=[smem(), hbm, hbm],
            out_specs=[vmem()] * 4,
            scratch_shapes=[
                pltpu.VMEM((2 * PICKED, rank, down_weight.shape[1]), bf16),
                pltpu.SemaphoreType.DMA((2 * PICKED,)),
            ],
            compiler_params=params(),
            name="cut_tiles",
        )(
            info,
            in_hbm(jnp.transpose(down_weight, (0, 2, 1))),
            in_hbm(jnp.transpose(up_weight, (0, 2, 1))),
        )

    def base_partials(me):
        parts = 4
        return pl.pallas_call(
            lambda *refs: base_kernel(tables, *refs),
            out_shape=[
                jax.ShapeDtypeStruct((positions, live_rows, width), bf16),
                jax.ShapeDtypeStruct((positions, live_rows, width), f32),
            ],
            in_specs=[smem(), vmem(), hbm],
            out_specs=[vmem()] * 2,
            scratch_shapes=[
                pltpu.VMEM((parts, width, output_weight.shape[1] // parts), bf16),
                pltpu.SemaphoreType.DMA((parts,)),
            ],
            compiler_params=params(),
            name="base_partials",
        )(me, live, in_hbm(output_weight))

    def shrink_start(i, x):
        return pl.pallas_call(
            lambda *refs: shrink_start_kernel(range(half), *refs),
            out_shape=jax.ShapeDtypeStruct((2, sizes[i], PICKED * rank), f32),
            in_specs=[vmem()] * 3,
            out_specs=vmem(),
            compiler_params=params(),
            name="shrink_start",
        )(x, down_own, down_peer)

    def shrink(i, sums, x):
        return pl.pallas_call(
            lambda *refs: shrink_kernel(starts[i], range(half, positions), *refs),
            out_shape=jax.ShapeDtypeStruct((sizes[i], rank), f32),
            in_specs=[vmem()] * 5,
            out_specs=vmem(),
            compiler_params=params(),
            name="shrink",
        )(code, sums, x, down_own, down_peer)

    def expand(i, part, dtype):
        return pl.pallas_call(
            lambda *refs: expand_kernel(
                starts[i], range(part * half, (part + 1) * half), *refs
            ),
            out_shape=jax.ShapeDtypeStruct((half, sizes[i], width), dtype),
            in_specs=[vmem()] * 7,
            out_specs=vmem(),
            compiler_params=params(),
            name="expand",
        )(code, mine[i], theirs[i], base_keep, base_got, up_own, up_peer)

    def swap(parts, masks):
        return [exchange(part, *mask) for part, mask in zip(parts, masks)]

    stages = len(groups)
    cut_at = max(stages - 2, 0)
    gathered = live[None]
    for k, masks in enumerate(groups):
        before = gathered
        if k < stages - 1:
            got = swap([gathered] * len(masks), masks)
            gathered = jnp.concatenate([gathered, *got], axis=0)
        else:
            gathered = [gathered[:, a : a + n] for a, n in zip(starts, sizes)]
            got = [exchange(part, *masks[0]) for part in gathered]
        if k == 0:
            down_send, down_own, up_send, up_own = cut_tiles(info)
            gathered, down_send, up_send, code = after((gathered, down_send, up_send, code))
            down_peer = exchange(down_send, 1, 1)
            up_peer = exchange(up_send, 1, 1)
        if k == cut_at:
            gathered, down_peer = after((gathered, down_peer))
        if k == cut_at:
            base_send, base_keep = base_partials(after(me, before))
            gathered, base_send = after((gathered, base_send))
            base_got = exchange(base_send, 1, 1)

    sums = [shrink_start(i, part) for i, part in enumerate(gathered)]

    got[0] = after(got[0], sums)
    mine, theirs, send = [None] * chains, [None] * chains, [None] * chains
    for i in range(chains):
        last = got[i] if i == 0 else after(got[i], send[i - 1])
        mine[i] = shrink(i, sums[i], last)
        theirs[i] = exchange(mine[i], 1, 1)
        send[i] = expand(i, 1, bf16)
    keep = [expand(i, 0, f32) for i in range(chains)]

    send = [[value] for value in send]
    for k, masks in reversed(list(enumerate(groups))):
        if k < stages - 1:
            total = [a + sum(part.astype(f32) for part in b) for a, b in zip(keep, got)]
            if k == 0:
                total = [jnp.concatenate(total, axis=1)]
            left = total[0].shape[0] // (len(masks) + 1)
            keep = [value[:left] for value in total]
            send = [
                [value[(j + 1) * left : (j + 2) * left].astype(bf16) for j in range(len(masks))]
                for value in total
            ]
        got = [swap(parts, masks) for parts in send]
    return pl.pallas_call(
        lambda *refs: spread_rows_kernel(len(keep), *refs),
        out_shape=jax.ShapeDtypeStruct((total_rows, width), bf16),
        in_specs=[vmem()] * (1 + len(keep) * (1 + len(groups[0]))),
        out_specs=vmem(),
        compiler_params=params(),
        name="spread_rows",
    )(pick, *keep, *[part for parts in got for part in parts])


def per_device(*arrays):
    width, features = arrays[0].shape[1], arrays[1].shape[1]
    if width % 128 == 0 and lax.axis_size("replica") >= 4:
        return owner_side(*arrays)
    return tile_side(*arrays)


def solution(mesh):
    in_specs = (
        P("parts", "replica"),
        P("replica", None),
        P(("parts", "replica"), None, None),
        P(("parts", "replica"), None, None),
        P("parts"),
        P("parts"),
        P("parts"),
    )
    out_specs = P("parts", "replica")
    return jax.shard_map(
        per_device, mesh=mesh, in_specs=in_specs, out_specs=out_specs, check_vma=False
    )
```

```python
import jax
import jax.numpy as jnp
from jax import lax
from jax.experimental import pallas as pl
from jax.experimental.pallas import tpu as pltpu
from jax.sharding import PartitionSpec as P

BLOCK = 4


ADAPTER_SCALE = 2.0

PICKED = 2

VMEM_LIMIT = 16 * 1024 * 1024


def segment_member(segment_rows, total_rows, block_rows):
    padded = (segment_rows + block_rows - 1) // block_rows * block_rows
    starts = jnp.cumsum(padded) - padded
    row_ids = jnp.arange(total_rows, dtype=jnp.int32)
    inside = (row_ids[:, None] >= starts[None, :]) & (
        row_ids[:, None] < (starts + segment_rows)[None, :]
    )
    return inside.astype(jnp.float32)


def slot_lookup(store_adapter_ids, segment_adapter):
    positions = jnp.arange(store_adapter_ids.shape[0], dtype=jnp.int32)
    equal = store_adapter_ids[None, :] == segment_adapter[:, None]
    return jnp.sum(jnp.where(equal, positions[None, :], 0), axis=1)


def tile_side(
    attention_output,
    output_weight,
    down_weight,
    up_weight,
    store_adapter_ids,
    segment_adapter,
    segment_rows,
):
    device_list = lax.axis_size("replica")
    total_rows, feature_columns = attention_output.shape
    holding_count, hidden_width, adapter_rank_size = down_weight.shape
    seg_count = segment_rows.shape[0]
    member = segment_member(segment_rows, total_rows, BLOCK)
    active_rows = jnp.sum(member, axis=1)
    slot_for_adapter = slot_lookup(store_adapter_ids, segment_adapter)
    partial_value = jnp.dot(attention_output, output_weight, preferred_element_type=jnp.float32)
    down_pieces = down_weight.reshape(
        holding_count, device_list, feature_columns, adapter_rank_size
    )
    up_pieces = up_weight.reshape(holding_count, device_list, feature_columns, adapter_rank_size)
    tile_pairs = jnp.concatenate([down_pieces, up_pieces], axis=3)
    arrived = lax.all_to_all(tile_pairs, "replica", split_axis=1, concat_axis=0, tiled=True)
    arrived = arrived.reshape(-1, feature_columns, 2 * adapter_rank_size)
    seg_tiles = arrived[slot_for_adapter]
    a_part = seg_tiles[:, :, :adapter_rank_size]
    b_part = seg_tiles[:, :, adapter_rank_size:]
    a_matrix = jnp.transpose(a_part, (1, 0, 2)).reshape(
        feature_columns, seg_count * adapter_rank_size
    )
    shrink_all = jnp.dot(attention_output, a_matrix, preferred_element_type=jnp.float32)
    shrink_all = shrink_all.reshape(total_rows, seg_count, adapter_rank_size)
    shrink_part = jnp.einsum("ps,psr->pr", member, shrink_all)
    base_column_block = lax.psum_scatter(partial_value, "replica", scatter_dimension=1, tiled=True)
    shrink = lax.psum(shrink_part, "replica")
    shrink_half = shrink.astype(jnp.bfloat16)
    spread = (member[:, :, None] * shrink_half.astype(jnp.float32)[:, None, :]).astype(jnp.bfloat16)
    spread = spread.reshape(total_rows, seg_count * adapter_rank_size)
    b_matrix = jnp.transpose(b_part, (0, 2, 1)).reshape(
        seg_count * adapter_rank_size, feature_columns
    )
    adapter_column_block = jnp.dot(spread, b_matrix, preferred_element_type=jnp.float32)
    mixed = active_rows[:, None] * (base_column_block + ADAPTER_SCALE * adapter_column_block)
    return mixed.astype(jnp.bfloat16)


def stage_masks(device_count):
    masks = []
    mask = device_count // 2
    while mask >= 2:
        masks.append(mask)
        mask //= 2
    other = list(masks)
    if len(other) >= 2:
        other[-1], other[-2] = other[-2], other[-1]
    return masks, other


def stage_groups(even, odd):
    pairs = list(zip(even, odd))
    groups = [pairs[:2]] + [[pair] for pair in pairs[2:]] if len(pairs) > 2 else [[p] for p in pairs]
    found = []
    for group in groups:
        masks = [(0, 0)]
        for even_mask, odd_mask in group:
            masks = masks + [(a ^ even_mask, b ^ odd_mask) for a, b in masks]
        found.append(masks[1:])
    return found


def turned(position, stages):
    high, low = 1 << (stages - 1), 1 << (stages - 2)
    rest = position & ~(high | low)
    return rest | (low if position & high else 0) | (high if position & low else 0)


def chain_rows(live_rows):
    return live_rows - live_rows // 2, live_rows // 2


def position_masks(masks):
    found = [0]
    for mask in masks:
        found = found + [value ^ mask for value in found]
    return found


def exchange(value, mask_even, mask_odd):
    count = lax.axis_size("replica")
    pairs = [(i, i ^ (mask_odd if i & 1 else mask_even)) for i in range(count)]
    return lax.ppermute(value, "replica", pairs)


def block_at(device, position, tables):
    even, odd = tables[0][position], tables[1][position]
    if even == odd:
        return jnp.bitwise_xor(device, even)
    return jnp.bitwise_xor(device, jnp.where(jnp.bitwise_and(device, 1) == 0, even, odd))


def padded_row(live_row, rows_ref):
    place = live_row
    end = jnp.int32(0)
    for s in range(rows_ref.shape[0]):
        count = rows_ref[s]
        gap = (BLOCK - count % BLOCK) % BLOCK
        end = end + count
        place = place + jnp.where(live_row >= end, gap, 0)
    return place


def compact_kernel(rows_hbm, x_hbm, wanted_hbm, store_hbm, *refs):
    out_ref, pick_ref, code_ref, slot_ref, rows_ref, x_ref, wanted_ref, store_ref, sems = refs
    rows_copy, x_copy, wanted_copy, store_copy = (
        pltpu.make_async_copy(source, target, sems.at[i])
        for i, (source, target) in enumerate(
            (
                (rows_hbm, rows_ref),
                (x_hbm, x_ref),
                (wanted_hbm, wanted_ref),
                (store_hbm, store_ref),
            )
        )
    )
    for copy in (rows_copy, x_copy, wanted_copy, store_copy):
        copy.start()
    rows_copy.wait()
    shape = (out_ref.shape[0], x_ref.shape[0])
    live_row = lax.broadcasted_iota(jnp.int32, shape, 0)
    layout_row = lax.broadcasted_iota(jnp.int32, shape, 1)
    pick = jnp.where(padded_row(live_row, rows_ref) == layout_row, 1.0, 0.0).astype(jnp.bfloat16)
    x_copy.wait()
    rows = jnp.dot(pick, x_ref[...], preferred_element_type=jnp.float32)
    out_ref[...] = rows.astype(jnp.bfloat16)
    shape = pick_ref.shape
    live_row = lax.broadcasted_iota(jnp.int32, shape, 1)
    layout_row = lax.broadcasted_iota(jnp.int32, shape, 0)
    back = padded_row(live_row, rows_ref) == layout_row
    pick_ref[...] = jnp.where(back, 1.0, 0.0).astype(jnp.bfloat16)
    live_row = lax.broadcasted_iota(jnp.int32, code_ref.shape, 0)
    segment = jnp.zeros(code_ref.shape, jnp.int32)
    end = jnp.int32(0)
    for s in range(rows_ref.shape[0] - 1):
        end = end + rows_ref[s]
        segment = segment + jnp.where(live_row >= end, 1, 0)
    code_ref[...] = segment
    wanted_copy.wait()
    store_copy.wait()
    shape = (wanted_ref.shape[0], store_ref.shape[1])
    row = lax.broadcasted_iota(jnp.int32, shape, 0)
    lane = lax.broadcasted_iota(jnp.int32, shape, 1)
    wanted = jnp.zeros(shape, jnp.int32)
    for s in range(shape[0]):
        wanted = jnp.where(row == s, wanted_ref[s], wanted)
    found = jnp.where(store_ref[...] == wanted, lane, 0).astype(jnp.float32)
    slot_ref[...] = jnp.broadcast_to(jnp.sum(found, axis=1, keepdims=True), slot_ref.shape)


def spread_rows_kernel(chains, pick_ref, *refs):
    keep_refs, got_refs, out_ref = refs[:chains], refs[chains:-1], refs[-1]
    each = len(got_refs) // chains
    live = []
    for i, keep_ref in enumerate(keep_refs):
        total = keep_ref[0]
        for got_ref in got_refs[i * each : (i + 1) * each]:
            total = total + got_ref[0].astype(jnp.float32)
        live.append(total.astype(jnp.bfloat16))
    mixed = live[0] if chains == 1 else jnp.concatenate(live, axis=0)
    out = jnp.dot(pick_ref[...], mixed, preferred_element_type=jnp.float32)
    out_ref[...] = out.astype(jnp.bfloat16)


def find_kernel(held, me_ref, slot_ref, segment_ref, info_ref, code_ref):
    me = me_ref[0]
    segs = slot_ref.shape[0]
    slot = slot_ref[:, :1]
    place = jnp.zeros((segs, 1), jnp.float32)
    for first, device in ((0, me), (PICKED, jnp.bitwise_xor(me, 1))):
        local = slot - (device * held).astype(jnp.float32)
        here = (local >= 0.0) & (local < held)
        low = jnp.minimum(jnp.min(jnp.where(here, local, float(held))), held - 1.0)
        place = jnp.where(here, jnp.where(local == low, first + 1.0, first + 2.0), place)
        if first == 0:
            info_ref[0] = me
            info_ref[1] = low.astype(jnp.int32)
            info_ref[2] = jnp.max(jnp.where(here, local, 0.0)).astype(jnp.int32)
    segment = segment_ref[...]
    code = jnp.zeros(segment.shape, jnp.float32)
    for s in range(segs):
        code = jnp.where(segment == s, place[s : s + 1, :], code)
    code_ref[...] = code


def base_kernel(tables, me_ref, x_ref, w_hbm, send_ref, keep_ref, w_ref, sems):
    me = me_ref[0]
    peer = jnp.bitwise_xor(me, 1)
    parts, group_width = w_ref.shape[0], w_ref.shape[2]
    width = x_ref.shape[1]
    group = group_width // width
    copies = []
    for g in range(parts):
        at = pl.multiple_of(jnp.bitwise_xor(me // group, g) * group_width, group_width)
        copies.append(
            pltpu.make_async_copy(w_hbm.at[:, pl.ds(at, group_width)], w_ref.at[g], sems.at[g])
        )
        copies[-1].start()
    x = x_ref[...]
    for g in range(parts):
        copies[g].wait()
        for p in range(len(tables[0])):
            if tables[0][p] // group != g:
                continue
            for device, out_ref in ((peer, send_ref), (me, keep_ref)):
                at = pl.multiple_of(block_at(device, p, tables) % group * width, width)
                part = jnp.dot(
                    x, w_ref[g, :, pl.ds(at, width)], preferred_element_type=jnp.float32
                )
                out_ref[p] = part.astype(out_ref.dtype)


def tiles_kernel(tables, info_ref, *refs):
    stores, outs, held_ref, sems = refs[:2], refs[2:6], refs[6], refs[7]
    me = info_ref[0]
    peer = jnp.bitwise_xor(me, 1)
    width = outs[0].shape[2]
    rank = stores[0].shape[1]
    copies = []
    for k, store in enumerate(stores):
        for j in range(PICKED):
            at = PICKED * k + j
            copies.append(
                pltpu.make_async_copy(store.at[info_ref[1 + j]], held_ref.at[at], sems.at[at])
            )
            copies[-1].start()
    for at, copy in enumerate(copies):
        copy.wait()
        k, j = at // PICKED, at % PICKED
        for p in range(len(tables[0])):
            for device, out in ((peer, outs[2 * k]), (me, outs[2 * k + 1])):
                lane = pl.multiple_of(block_at(device, p, tables) * width, width)
                out[p, j * rank : (j + 1) * rank, :] = held_ref[at, :, pl.ds(lane, width)]


def shrink_sums(places, x_ref, own_ref, peer_ref, own, peer):
    contract = (((1,), (1,)), ((), ()))
    for p, at in enumerate(places):
        x = x_ref[p]
        own = own + lax.dot_general(x, own_ref[at], contract, preferred_element_type=jnp.float32)
        peer = peer + lax.dot_general(x, peer_ref[at], contract, preferred_element_type=jnp.float32)
    return own, peer


def shrink_start_kernel(places, x_ref, own_ref, peer_ref, out_ref):
    zero = jnp.zeros(out_ref.shape[1:], jnp.float32)
    out_ref[0], out_ref[1] = shrink_sums(places, x_ref, own_ref, peer_ref, zero, zero)


def shrink_kernel(row, places, code_ref, sums_ref, x_ref, own_ref, peer_ref, out_ref):
    rows, rank = out_ref.shape
    sums = shrink_sums(places, x_ref, own_ref, peer_ref, sums_ref[0], sums_ref[1])
    code = code_ref[row : row + rows, :]
    total = jnp.zeros((rows, rank), jnp.float32)
    for place, part in enumerate(sums):
        for j in range(PICKED):
            value = part[:, j * rank : (j + 1) * rank]
            total = total + jnp.where(code == 1 + place * PICKED + j, value, 0.0)
    out_ref[...] = total


def expand_kernel(
    row, places, code_ref, mine_ref, got_ref, keep_ref, base_ref, own_ref, peer_ref, out_ref
):
    rows = out_ref.shape[1]
    half = (mine_ref[...] + got_ref[...]).astype(jnp.bfloat16)
    code = code_ref[row : row + rows, :]
    picked = [
        jnp.where(code == 1 + j, half.astype(jnp.float32), 0.0).astype(jnp.bfloat16)
        for j in range(2 * PICKED)
    ]
    own = jnp.concatenate(picked[:PICKED], axis=1)
    peer = jnp.concatenate(picked[PICKED:], axis=1)
    for p, at in enumerate(places):
        term = jnp.dot(own, own_ref[at], preferred_element_type=jnp.float32)
        term = term + jnp.dot(peer, peer_ref[at], preferred_element_type=jnp.float32)
        base = keep_ref[at, row : row + rows] + base_ref[at, row : row + rows].astype(jnp.float32)
        out_ref[p] = (base + ADAPTER_SCALE * term).astype(out_ref.dtype)


def after(values, *earlier):
    return lax.optimization_barrier((values, earlier))[0]


def smem():
    return pl.BlockSpec(memory_space=pltpu.SMEM)


def vmem():
    return pl.BlockSpec(memory_space=pltpu.VMEM)


def in_hbm(value):
    return pltpu.with_memory_space_constraint(value, pltpu.HBM)


def params(**more):
    return pltpu.CompilerParams(vmem_limit_bytes=VMEM_LIMIT, **more)


def owner_side(
    attention_output,
    output_weight,
    down_weight,
    up_weight,
    store_adapter_ids,
    segment_adapter,
    segment_rows,
):
    bf16, f32 = jnp.bfloat16, jnp.float32
    device_count = lax.axis_size("replica")
    me = lax.axis_index("replica")
    total_rows, width = attention_output.shape
    held, _, rank = down_weight.shape
    seg_count = segment_rows.shape[0]
    live_rows = total_rows - seg_count * (BLOCK - 1)
    sizes = chain_rows(live_rows)
    chains = len(sizes)
    starts = [sum(sizes[:i]) for i in range(chains)]
    even_masks, odd_masks = stage_masks(device_count)
    tables = (position_masks(even_masks), position_masks(odd_masks))
    positions = len(tables[0])
    half = positions // 2
    groups = stage_groups(even_masks, odd_masks)
    plain = list(range(positions))
    orders, places = [groups] * chains, [plain] * chains
    if len(groups) > 2:
        other = groups[:-2] + groups[-2:][::-1]
        moved = [turned(p, len(even_masks)) for p in plain]
        orders = [other if i % 2 else groups for i in range(chains)]
        places = [moved if i % 2 else plain for i in range(chains)]

    me = jnp.reshape(me, (1,))

    hbm = pl.BlockSpec(memory_space=pltpu.HBM)
    live, pick, segment, slots = pl.pallas_call(
        compact_kernel,
        out_shape=[
            jax.ShapeDtypeStruct((live_rows, width), bf16),
            jax.ShapeDtypeStruct((total_rows, live_rows), bf16),
            jax.ShapeDtypeStruct((live_rows, rank), jnp.int32),
            jax.ShapeDtypeStruct((seg_count, 128), f32),
        ],
        in_specs=[hbm] * 4,
        out_specs=[vmem()] * 4,
        scratch_shapes=[
            pltpu.SMEM(segment_rows.shape, jnp.int32),
            pltpu.VMEM(attention_output.shape, bf16),
            pltpu.SMEM(segment_adapter.shape, jnp.int32),
            pltpu.VMEM((1, store_adapter_ids.shape[0]), jnp.int32),
            pltpu.SemaphoreType.DMA((4,)),
        ],
        compiler_params=params(),
        name="compact_rows",
    )(
        in_hbm(segment_rows),
        in_hbm(attention_output),
        in_hbm(segment_adapter),
        in_hbm(jnp.reshape(store_adapter_ids, (1, -1))),
    )

    info, code = pl.pallas_call(
        lambda *refs: find_kernel(held, *refs),
        out_shape=[
            jax.ShapeDtypeStruct((1 + PICKED,), jnp.int32),
            jax.ShapeDtypeStruct((live_rows, rank), f32),
        ],
        in_specs=[smem(), vmem(), vmem()],
        out_specs=[smem(), vmem()],
        compiler_params=params(),
        name="find_adapters",
    )(me, slots, segment)

    def cut_tiles(info):
        return pl.pallas_call(
            lambda *refs: tiles_kernel(tables, *refs),
            out_shape=[jax.ShapeDtypeStruct((positions, PICKED * rank, width), bf16)] * 4,
            in_specs=[smem(), hbm, hbm],
            out_specs=[vmem()] * 4,
            scratch_shapes=[
                pltpu.VMEM((2 * PICKED, rank, down_weight.shape[1]), bf16),
                pltpu.SemaphoreType.DMA((2 * PICKED,)),
            ],
            compiler_params=params(),
            name="cut_tiles",
        )(
            info,
            in_hbm(jnp.transpose(down_weight, (0, 2, 1))),
            in_hbm(jnp.transpose(up_weight, (0, 2, 1))),
        )

    def base_partials(me):
        parts = 4
        return pl.pallas_call(
            lambda *refs: base_kernel(tables, *refs),
            out_shape=[
                jax.ShapeDtypeStruct((positions, live_rows, width), bf16),
                jax.ShapeDtypeStruct((positions, live_rows, width), f32),
            ],
            in_specs=[smem(), vmem(), hbm],
            out_specs=[vmem()] * 2,
            scratch_shapes=[
                pltpu.VMEM((parts, width, output_weight.shape[1] // parts), bf16),
                pltpu.SemaphoreType.DMA((parts,)),
            ],
            compiler_params=params(),
            name="base_partials",
        )(me, live, in_hbm(output_weight))

    def shrink_start(i, x):
        return pl.pallas_call(
            lambda *refs: shrink_start_kernel(range(half), *refs),
            out_shape=jax.ShapeDtypeStruct((2, sizes[i], PICKED * rank), f32),
            in_specs=[vmem()] * 3,
            out_specs=vmem(),
            compiler_params=params(),
            name="shrink_start",
        )(x, down_own, down_peer)

    def shrink(i, sums, x):
        return pl.pallas_call(
            lambda *refs: shrink_kernel(starts[i], range(half, positions), *refs),
            out_shape=jax.ShapeDtypeStruct((sizes[i], rank), f32),
            in_specs=[vmem()] * 5,
            out_specs=vmem(),
            compiler_params=params(),
            name="shrink",
        )(code, sums, x, down_own, down_peer)

    def expand(i, part, dtype):
        return pl.pallas_call(
            lambda *refs: expand_kernel(
                starts[i], places[i][part * half : (part + 1) * half], *refs
            ),
            out_shape=jax.ShapeDtypeStruct((half, sizes[i], width), dtype),
            in_specs=[vmem()] * 7,
            out_specs=vmem(),
            compiler_params=params(),
            name="expand",
        )(code, mine[i], theirs[i], base_keep, base_got, up_own, up_peer)

    def swap(parts, masks):
        return [exchange(part, *mask) for part, mask in zip(parts, masks)]

    stages = len(groups)
    cut_at = max(stages - 2, 0)
    gathered = live[None]
    for k, masks in enumerate(groups):
        before = gathered
        if k < stages - 1:
            got = swap([gathered] * len(masks), masks)
            gathered = jnp.concatenate([gathered, *got], axis=0)
        else:
            gathered = [gathered[:, a : a + n] for a, n in zip(starts, sizes)]
            got = [exchange(part, *masks[0]) for part in gathered]
        if k == 0:
            down_send, down_own, up_send, up_own = cut_tiles(info)
            gathered, down_send, up_send, code = after((gathered, down_send, up_send, code))
            down_peer = exchange(down_send, 1, 1)
            up_peer = exchange(up_send, 1, 1)
        if k == cut_at:
            gathered, down_peer = after((gathered, down_peer))
        if k == cut_at:
            base_send, base_keep = base_partials(after(me, before))
            gathered, base_send = after((gathered, base_send))
            base_got = exchange(base_send, 1, 1)

    sums = [shrink_start(i, part) for i, part in enumerate(gathered)]

    got[0] = after(got[0], sums)
    mine, theirs, send = [None] * chains, [None] * chains, [None] * chains
    for i in range(chains):
        last = got[i] if i == 0 else after(got[i], send[i - 1])
        mine[i] = shrink(i, sums[i], last)
        theirs[i] = exchange(mine[i], 1, 1)
        send[i] = expand(i, 1, bf16)
    keep = [expand(i, 0, f32) for i in range(chains)]

    send = [[value] for value in send]
    for k, masks in reversed(list(enumerate(groups))):
        if k < stages - 1:
            total = [a + sum(part.astype(f32) for part in b) for a, b in zip(keep, got)]
            if k == 0:
                total = [jnp.concatenate(total, axis=1)]
            left = total[0].shape[0] // (len(masks) + 1)
            keep = [value[:left] for value in total]
            send = [
                [value[(j + 1) * left : (j + 2) * left].astype(bf16) for j in range(len(masks))]
                for value in total
            ]
        got = [swap(parts, order[k]) for parts, order in zip(send, orders)]
    return pl.pallas_call(
        lambda *refs: spread_rows_kernel(len(keep), *refs),
        out_shape=jax.ShapeDtypeStruct((total_rows, width), bf16),
        in_specs=[vmem()] * (1 + len(keep) * (1 + len(groups[0]))),
        out_specs=vmem(),
        compiler_params=params(),
        name="spread_rows",
    )(pick, *keep, *[part for parts in got for part in parts])


def per_device(*arrays):
    width, features = arrays[0].shape[1], arrays[1].shape[1]
    if width % 128 == 0 and lax.axis_size("replica") >= 4:
        return owner_side(*arrays)
    return tile_side(*arrays)


def solution(mesh):
    in_specs = (
        P("parts", "replica"),
        P("replica", None),
        P(("parts", "replica"), None, None),
        P(("parts", "replica"), None, None),
        P("parts"),
        P("parts"),
        P("parts"),
    )
    out_specs = P("parts", "replica")
    return jax.shard_map(
        per_device, mesh=mesh, in_specs=in_specs, out_specs=out_specs, check_vma=False
    )
```

```python
import jax
import jax.numpy as jnp
from jax import lax
from jax.experimental import pallas as pl
from jax.experimental.pallas import tpu as pltpu
from jax.sharding import PartitionSpec as P

BLOCK = 4


ADAPTER_SCALE = 2.0

PICKED = 2

VMEM_LIMIT = 16 * 1024 * 1024


def segment_member(segment_rows, total_rows, block_rows):
    padded = (segment_rows + block_rows - 1) // block_rows * block_rows
    starts = jnp.cumsum(padded) - padded
    row_ids = jnp.arange(total_rows, dtype=jnp.int32)
    inside = (row_ids[:, None] >= starts[None, :]) & (
        row_ids[:, None] < (starts + segment_rows)[None, :]
    )
    return inside.astype(jnp.float32)


def slot_lookup(store_adapter_ids, segment_adapter):
    positions = jnp.arange(store_adapter_ids.shape[0], dtype=jnp.int32)
    equal = store_adapter_ids[None, :] == segment_adapter[:, None]
    return jnp.sum(jnp.where(equal, positions[None, :], 0), axis=1)


def tile_side(
    attention_output,
    output_weight,
    down_weight,
    up_weight,
    store_adapter_ids,
    segment_adapter,
    segment_rows,
):
    device_list = lax.axis_size("replica")
    total_rows, feature_columns = attention_output.shape
    holding_count, hidden_width, adapter_rank_size = down_weight.shape
    seg_count = segment_rows.shape[0]
    member = segment_member(segment_rows, total_rows, BLOCK)
    active_rows = jnp.sum(member, axis=1)
    slot_for_adapter = slot_lookup(store_adapter_ids, segment_adapter)
    partial_value = jnp.dot(attention_output, output_weight, preferred_element_type=jnp.float32)
    down_pieces = down_weight.reshape(
        holding_count, device_list, feature_columns, adapter_rank_size
    )
    up_pieces = up_weight.reshape(holding_count, device_list, feature_columns, adapter_rank_size)
    tile_pairs = jnp.concatenate([down_pieces, up_pieces], axis=3)
    arrived = lax.all_to_all(tile_pairs, "replica", split_axis=1, concat_axis=0, tiled=True)
    arrived = arrived.reshape(-1, feature_columns, 2 * adapter_rank_size)
    seg_tiles = arrived[slot_for_adapter]
    a_part = seg_tiles[:, :, :adapter_rank_size]
    b_part = seg_tiles[:, :, adapter_rank_size:]
    a_matrix = jnp.transpose(a_part, (1, 0, 2)).reshape(
        feature_columns, seg_count * adapter_rank_size
    )
    shrink_all = jnp.dot(attention_output, a_matrix, preferred_element_type=jnp.float32)
    shrink_all = shrink_all.reshape(total_rows, seg_count, adapter_rank_size)
    shrink_part = jnp.einsum("ps,psr->pr", member, shrink_all)
    base_column_block = lax.psum_scatter(partial_value, "replica", scatter_dimension=1, tiled=True)
    shrink = lax.psum(shrink_part, "replica")
    shrink_half = shrink.astype(jnp.bfloat16)
    spread = (member[:, :, None] * shrink_half.astype(jnp.float32)[:, None, :]).astype(jnp.bfloat16)
    spread = spread.reshape(total_rows, seg_count * adapter_rank_size)
    b_matrix = jnp.transpose(b_part, (0, 2, 1)).reshape(
        seg_count * adapter_rank_size, feature_columns
    )
    adapter_column_block = jnp.dot(spread, b_matrix, preferred_element_type=jnp.float32)
    mixed = active_rows[:, None] * (base_column_block + ADAPTER_SCALE * adapter_column_block)
    return mixed.astype(jnp.bfloat16)


def stage_masks(device_count):
    masks = []
    mask = device_count // 2
    while mask >= 2:
        masks.append(mask)
        mask //= 2
    other = list(masks)
    if len(other) >= 2:
        other[-1], other[-2] = other[-2], other[-1]
    return masks, other


def stage_groups(even, odd):
    pairs = list(zip(even, odd))
    groups = [pairs[:2]] + [[pair] for pair in pairs[2:]] if len(pairs) > 2 else [[p] for p in pairs]
    found = []
    for group in groups:
        masks = [(0, 0)]
        for even_mask, odd_mask in group:
            masks = masks + [(a ^ even_mask, b ^ odd_mask) for a, b in masks]
        found.append(masks[1:])
    return found


def turned(position, stages):
    high, low = 1 << (stages - 1), 1 << (stages - 2)
    rest = position & ~(high | low)
    return rest | (low if position & high else 0) | (high if position & low else 0)


def chain_rows(live_rows):
    return live_rows - live_rows // 2, live_rows // 2


def position_masks(masks):
    found = [0]
    for mask in masks:
        found = found + [value ^ mask for value in found]
    return found


def exchange(value, mask_even, mask_odd):
    count = lax.axis_size("replica")
    pairs = [(i, i ^ (mask_odd if i & 1 else mask_even)) for i in range(count)]
    return lax.ppermute(value, "replica", pairs)


def block_at(device, position, tables):
    even, odd = tables[0][position], tables[1][position]
    if even == odd:
        return jnp.bitwise_xor(device, even)
    return jnp.bitwise_xor(device, jnp.where(jnp.bitwise_and(device, 1) == 0, even, odd))


def padded_row(live_row, rows_ref):
    place = live_row
    end = jnp.int32(0)
    for s in range(rows_ref.shape[0]):
        count = rows_ref[s]
        gap = (BLOCK - count % BLOCK) % BLOCK
        end = end + count
        place = place + jnp.where(live_row >= end, gap, 0)
    return place


def compact_kernel(rows_hbm, x_hbm, wanted_hbm, store_hbm, *refs):
    out_ref, pick_ref, code_ref, slot_ref, rows_ref, x_ref, wanted_ref, store_ref, sems = refs
    rows_copy, x_copy, wanted_copy, store_copy = (
        pltpu.make_async_copy(source, target, sems.at[i])
        for i, (source, target) in enumerate(
            (
                (rows_hbm, rows_ref),
                (x_hbm, x_ref),
                (wanted_hbm, wanted_ref),
                (store_hbm, store_ref),
            )
        )
    )
    for copy in (rows_copy, x_copy, wanted_copy, store_copy):
        copy.start()
    rows_copy.wait()
    shape = (out_ref.shape[0], x_ref.shape[0])
    live_row = lax.broadcasted_iota(jnp.int32, shape, 0)
    layout_row = lax.broadcasted_iota(jnp.int32, shape, 1)
    pick = jnp.where(padded_row(live_row, rows_ref) == layout_row, 1.0, 0.0).astype(jnp.bfloat16)
    x_copy.wait()
    rows = jnp.dot(pick, x_ref[...], preferred_element_type=jnp.float32)
    out_ref[...] = rows.astype(jnp.bfloat16)
    shape = pick_ref.shape
    live_row = lax.broadcasted_iota(jnp.int32, shape, 1)
    layout_row = lax.broadcasted_iota(jnp.int32, shape, 0)
    back = padded_row(live_row, rows_ref) == layout_row
    pick_ref[...] = jnp.where(back, 1.0, 0.0).astype(jnp.bfloat16)
    live_row = lax.broadcasted_iota(jnp.int32, code_ref.shape, 0)
    segment = jnp.zeros(code_ref.shape, jnp.int32)
    end = jnp.int32(0)
    for s in range(rows_ref.shape[0] - 1):
        end = end + rows_ref[s]
        segment = segment + jnp.where(live_row >= end, 1, 0)
    code_ref[...] = segment
    wanted_copy.wait()
    store_copy.wait()
    shape = (wanted_ref.shape[0], store_ref.shape[1])
    row = lax.broadcasted_iota(jnp.int32, shape, 0)
    lane = lax.broadcasted_iota(jnp.int32, shape, 1)
    wanted = jnp.zeros(shape, jnp.int32)
    for s in range(shape[0]):
        wanted = jnp.where(row == s, wanted_ref[s], wanted)
    found = jnp.where(store_ref[...] == wanted, lane, 0).astype(jnp.float32)
    slot_ref[...] = jnp.broadcast_to(jnp.sum(found, axis=1, keepdims=True), slot_ref.shape)


def spread_rows_kernel(chains, pick_ref, *refs):
    keep_refs, got_refs, out_ref = refs[:chains], refs[chains:-1], refs[-1]
    each = len(got_refs) // chains
    live = []
    for i, keep_ref in enumerate(keep_refs):
        total = keep_ref[0]
        for got_ref in got_refs[i * each : (i + 1) * each]:
            total = total + got_ref[0].astype(jnp.float32)
        live.append(total.astype(jnp.bfloat16))
    mixed = live[0] if chains == 1 else jnp.concatenate(live, axis=0)
    out = jnp.dot(pick_ref[...], mixed, preferred_element_type=jnp.float32)
    out_ref[...] = out.astype(jnp.bfloat16)


def find_kernel(held, me_ref, slot_ref, segment_ref, info_ref, code_ref):
    me = me_ref[0]
    segs = slot_ref.shape[0]
    slot = slot_ref[:, :1]
    place = jnp.zeros((segs, 1), jnp.float32)
    for first, device in ((0, me), (PICKED, jnp.bitwise_xor(me, 1))):
        local = slot - (device * held).astype(jnp.float32)
        here = (local >= 0.0) & (local < held)
        low = jnp.minimum(jnp.min(jnp.where(here, local, float(held))), held - 1.0)
        place = jnp.where(here, jnp.where(local == low, first + 1.0, first + 2.0), place)
        if first == 0:
            info_ref[0] = me
            info_ref[1] = low.astype(jnp.int32)
            info_ref[2] = jnp.max(jnp.where(here, local, 0.0)).astype(jnp.int32)
    segment = segment_ref[...]
    code = jnp.zeros(segment.shape, jnp.float32)
    for s in range(segs):
        code = jnp.where(segment == s, place[s : s + 1, :], code)
    code_ref[...] = code


def base_kernel(tables, me_ref, x_ref, w_hbm, send_ref, keep_ref, w_ref, sems):
    me = me_ref[0]
    peer = jnp.bitwise_xor(me, 1)
    parts, group_width = w_ref.shape[0], w_ref.shape[2]
    width = x_ref.shape[1]
    group = group_width // width
    copies = []
    for g in range(parts):
        at = pl.multiple_of(jnp.bitwise_xor(me // group, g) * group_width, group_width)
        copies.append(
            pltpu.make_async_copy(w_hbm.at[:, pl.ds(at, group_width)], w_ref.at[g], sems.at[g])
        )
        copies[-1].start()
    x = x_ref[...]
    for g in range(parts):
        copies[g].wait()
        for p in range(len(tables[0])):
            if tables[0][p] // group != g:
                continue
            for device, out_ref in ((peer, send_ref), (me, keep_ref)):
                at = pl.multiple_of(block_at(device, p, tables) % group * width, width)
                part = jnp.dot(
                    x, w_ref[g, :, pl.ds(at, width)], preferred_element_type=jnp.float32
                )
                out_ref[p] = part.astype(out_ref.dtype)


def tiles_kernel(tables, info_ref, *refs):
    stores, outs, held_ref, sems = refs[:2], refs[2:6], refs[6], refs[7]
    me = info_ref[0]
    peer = jnp.bitwise_xor(me, 1)
    width = outs[0].shape[2]
    rank = stores[0].shape[1]
    copies = []
    for k, store in enumerate(stores):
        for j in range(PICKED):
            at = PICKED * k + j
            copies.append(
                pltpu.make_async_copy(store.at[info_ref[1 + j]], held_ref.at[at], sems.at[at])
            )
            copies[-1].start()
    for at, copy in enumerate(copies):
        copy.wait()
        k, j = at // PICKED, at % PICKED
        for p in range(len(tables[0])):
            for device, out in ((peer, outs[2 * k]), (me, outs[2 * k + 1])):
                lane = pl.multiple_of(block_at(device, p, tables) * width, width)
                out[p, j * rank : (j + 1) * rank, :] = held_ref[at, :, pl.ds(lane, width)]


def shrink_sums(places, x_ref, own_ref, peer_ref, own, peer):
    contract = (((1,), (1,)), ((), ()))
    for p, at in enumerate(places):
        x = x_ref[p]
        own = own + lax.dot_general(x, own_ref[at], contract, preferred_element_type=jnp.float32)
        peer = peer + lax.dot_general(x, peer_ref[at], contract, preferred_element_type=jnp.float32)
    return own, peer


def shrink_start_kernel(places, x_ref, own_ref, peer_ref, out_ref):
    zero = jnp.zeros(out_ref.shape[1:], jnp.float32)
    out_ref[0], out_ref[1] = shrink_sums(places, x_ref, own_ref, peer_ref, zero, zero)


def shrink_kernel(row, places, code_ref, sums_ref, x_ref, own_ref, peer_ref, out_ref):
    rows, rank = out_ref.shape
    sums = shrink_sums(places, x_ref, own_ref, peer_ref, sums_ref[0], sums_ref[1])
    code = code_ref[row : row + rows, :]
    total = jnp.zeros((rows, rank), jnp.float32)
    for place, part in enumerate(sums):
        for j in range(PICKED):
            value = part[:, j * rank : (j + 1) * rank]
            total = total + jnp.where(code == 1 + place * PICKED + j, value, 0.0)
    out_ref[...] = total


def expand_kernel(
    row, places, code_ref, mine_ref, got_ref, keep_ref, base_ref, own_ref, peer_ref, out_ref
):
    rows = out_ref.shape[1]
    half = (mine_ref[...] + got_ref[...]).astype(jnp.bfloat16)
    code = code_ref[row : row + rows, :]
    picked = [
        jnp.where(code == 1 + j, half.astype(jnp.float32), 0.0).astype(jnp.bfloat16)
        for j in range(2 * PICKED)
    ]
    own = jnp.concatenate(picked[:PICKED], axis=1)
    peer = jnp.concatenate(picked[PICKED:], axis=1)
    for p, at in enumerate(places):
        term = jnp.dot(own, own_ref[at], preferred_element_type=jnp.float32)
        term = term + jnp.dot(peer, peer_ref[at], preferred_element_type=jnp.float32)
        base = keep_ref[at, row : row + rows] + base_ref[at, row : row + rows].astype(jnp.float32)
        out_ref[p] = (base + ADAPTER_SCALE * term).astype(out_ref.dtype)


def after(values, *earlier):
    return lax.optimization_barrier((values, earlier))[0]


def smem():
    return pl.BlockSpec(memory_space=pltpu.SMEM)


def vmem():
    return pl.BlockSpec(memory_space=pltpu.VMEM)


def in_hbm(value):
    return pltpu.with_memory_space_constraint(value, pltpu.HBM)


def params(**more):
    return pltpu.CompilerParams(vmem_limit_bytes=VMEM_LIMIT, **more)


def owner_side(
    attention_output,
    output_weight,
    down_weight,
    up_weight,
    store_adapter_ids,
    segment_adapter,
    segment_rows,
):
    bf16, f32 = jnp.bfloat16, jnp.float32
    device_count = lax.axis_size("replica")
    me = lax.axis_index("replica")
    total_rows, width = attention_output.shape
    held, _, rank = down_weight.shape
    seg_count = segment_rows.shape[0]
    live_rows = total_rows - seg_count * (BLOCK - 1)
    sizes = chain_rows(live_rows)
    chains = len(sizes)
    starts = [sum(sizes[:i]) for i in range(chains)]
    even_masks, odd_masks = stage_masks(device_count)
    tables = (position_masks(even_masks), position_masks(odd_masks))
    positions = len(tables[0])
    half = positions // 2
    groups = stage_groups(even_masks, odd_masks)
    plain = list(range(positions))
    orders, places = [groups] * chains, [plain] * chains
    if len(groups) > 2:
        other = groups[:-2] + groups[-2:][::-1]
        moved = [turned(p, len(even_masks)) for p in plain]
        orders = [other if i % 2 else groups for i in range(chains)]
        places = [moved if i % 2 else plain for i in range(chains)]

    me = jnp.reshape(me, (1,))

    hbm = pl.BlockSpec(memory_space=pltpu.HBM)
    live, pick, segment, slots = pl.pallas_call(
        compact_kernel,
        out_shape=[
            jax.ShapeDtypeStruct((live_rows, width), bf16),
            jax.ShapeDtypeStruct((total_rows, live_rows), bf16),
            jax.ShapeDtypeStruct((live_rows, rank), jnp.int32),
            jax.ShapeDtypeStruct((seg_count, 128), f32),
        ],
        in_specs=[hbm] * 4,
        out_specs=[vmem()] * 4,
        scratch_shapes=[
            pltpu.SMEM(segment_rows.shape, jnp.int32),
            pltpu.VMEM(attention_output.shape, bf16),
            pltpu.SMEM(segment_adapter.shape, jnp.int32),
            pltpu.VMEM((1, store_adapter_ids.shape[0]), jnp.int32),
            pltpu.SemaphoreType.DMA((4,)),
        ],
        compiler_params=params(),
        name="compact_rows",
    )(
        in_hbm(segment_rows),
        in_hbm(attention_output),
        in_hbm(segment_adapter),
        in_hbm(jnp.reshape(store_adapter_ids, (1, -1))),
    )

    info, code = pl.pallas_call(
        lambda *refs: find_kernel(held, *refs),
        out_shape=[
            jax.ShapeDtypeStruct((1 + PICKED,), jnp.int32),
            jax.ShapeDtypeStruct((live_rows, rank), f32),
        ],
        in_specs=[smem(), vmem(), vmem()],
        out_specs=[smem(), vmem()],
        compiler_params=params(),
        name="find_adapters",
    )(me, slots, segment)

    def cut_tiles(info):
        return pl.pallas_call(
            lambda *refs: tiles_kernel(tables, *refs),
            out_shape=[jax.ShapeDtypeStruct((positions, PICKED * rank, width), bf16)] * 4,
            in_specs=[smem(), hbm, hbm],
            out_specs=[vmem()] * 4,
            scratch_shapes=[
                pltpu.VMEM((2 * PICKED, rank, down_weight.shape[1]), bf16),
                pltpu.SemaphoreType.DMA((2 * PICKED,)),
            ],
            compiler_params=params(),
            name="cut_tiles",
        )(
            info,
            in_hbm(jnp.transpose(down_weight, (0, 2, 1))),
            in_hbm(jnp.transpose(up_weight, (0, 2, 1))),
        )

    def base_partials(me):
        parts = 4
        return pl.pallas_call(
            lambda *refs: base_kernel(tables, *refs),
            out_shape=[
                jax.ShapeDtypeStruct((positions, live_rows, width), bf16),
                jax.ShapeDtypeStruct((positions, live_rows, width), f32),
            ],
            in_specs=[smem(), vmem(), hbm],
            out_specs=[vmem()] * 2,
            scratch_shapes=[
                pltpu.VMEM((parts, width, output_weight.shape[1] // parts), bf16),
                pltpu.SemaphoreType.DMA((parts,)),
            ],
            compiler_params=params(),
            name="base_partials",
        )(me, live, in_hbm(output_weight))

    def shrink_start(i, x):
        return pl.pallas_call(
            lambda *refs: shrink_start_kernel(range(half), *refs),
            out_shape=jax.ShapeDtypeStruct((2, sizes[i], PICKED * rank), f32),
            in_specs=[vmem()] * 3,
            out_specs=vmem(),
            compiler_params=params(),
            name="shrink_start",
        )(x, down_own, down_peer)

    def shrink(i, sums, x):
        return pl.pallas_call(
            lambda *refs: shrink_kernel(starts[i], range(half, positions), *refs),
            out_shape=jax.ShapeDtypeStruct((sizes[i], rank), f32),
            in_specs=[vmem()] * 5,
            out_specs=vmem(),
            compiler_params=params(),
            name="shrink",
        )(code, sums, x, down_own, down_peer)

    def expand(i, part, dtype):
        return pl.pallas_call(
            lambda *refs: expand_kernel(
                starts[i], places[i][part * half : (part + 1) * half], *refs
            ),
            out_shape=jax.ShapeDtypeStruct((half, sizes[i], width), dtype),
            in_specs=[vmem()] * 7,
            out_specs=vmem(),
            compiler_params=params(),
            name="expand",
        )(code, mine[i], theirs[i], base_keep, base_got, up_own, up_peer)

    def swap(parts, masks):
        return [exchange(part, *mask) for part, mask in zip(parts, masks)]

    stages = len(groups)
    cut_at = max(stages - 2, 0)
    gathered = live[None]
    for k, masks in enumerate(groups):
        before = gathered
        if k < stages - 1:
            got = swap([gathered] * len(masks), masks)
            gathered = jnp.concatenate([gathered, *got], axis=0)
        else:
            gathered = [gathered[:, a : a + n] for a, n in zip(starts, sizes)]
            got = [exchange(part, *masks[0]) for part in gathered]
        if k == 0:
            down_send, down_own, up_send, up_own = cut_tiles(info)
            gathered, down_send, up_send, code = after((gathered, down_send, up_send, code))
            down_peer = exchange(down_send, 1, 1)
            up_peer = exchange(up_send, 1, 1)
        if k == cut_at:
            base_send, base_keep = base_partials(after(me, before))
            gathered, base_send = after((gathered, base_send))
            base_got = exchange(base_send, 1, 1)

    sums = [shrink_start(i, part) for i, part in enumerate(gathered)]

    got[0] = after(got[0], sums)
    mine, theirs, send = [None] * chains, [None] * chains, [None] * chains
    for i in range(chains):
        last = got[i] if i == 0 else after(got[i], send[i - 1])
        mine[i] = shrink(i, sums[i], last)
        theirs[i] = exchange(mine[i], 1, 1)
        send[i] = expand(i, 1, bf16)
    keep = [expand(i, 0, f32) for i in range(chains)]

    send = [[value] for value in send]
    for k, masks in reversed(list(enumerate(groups))):
        if k < stages - 1:
            total = [a + sum(part.astype(f32) for part in b) for a, b in zip(keep, got)]
            if k == 0:
                total = [jnp.concatenate(total, axis=1)]
            left = total[0].shape[0] // (len(masks) + 1)
            keep = [value[:left] for value in total]
            send = [
                [value[(j + 1) * left : (j + 2) * left].astype(bf16) for j in range(len(masks))]
                for value in total
            ]
        got = [swap(parts, order[k]) for parts, order in zip(send, orders)]
    return pl.pallas_call(
        lambda *refs: spread_rows_kernel(len(keep), *refs),
        out_shape=jax.ShapeDtypeStruct((total_rows, width), bf16),
        in_specs=[vmem()] * (1 + len(keep) * (1 + len(groups[0]))),
        out_specs=vmem(),
        compiler_params=params(),
        name="spread_rows",
    )(pick, *keep, *[part for parts in got for part in parts])


def per_device(*arrays):
    width, features = arrays[0].shape[1], arrays[1].shape[1]
    if width % 128 == 0 and lax.axis_size("replica") >= 4:
        return owner_side(*arrays)
    return tile_side(*arrays)


def solution(mesh):
    in_specs = (
        P("parts", "replica"),
        P("replica", None),
        P(("parts", "replica"), None, None),
        P(("parts", "replica"), None, None),
        P("parts"),
        P("parts"),
        P("parts"),
    )
    out_specs = P("parts", "replica")
    return jax.shard_map(
        per_device, mesh=mesh, in_specs=in_specs, out_specs=out_specs, check_vma=False
    )
```
